256 devices in a mesh: expert: 64 (over y, z, core), dp: 4 (over x).
Axes of the slice: x: 4, y: 4, z: 8, core: 2. Of those that a mesh axis runs over, the one named last changes fastest.
Arguments:
- tokens: bfloat16 [32768, 2048], P(('expert', 'dp')), may hold values from -6 to 6
- out_grad: bfloat16 [32768, 2048], P(('expert', 'dp')), may hold values from -6 to 6
- expert_ids: int32 [32768, 8], P(('expert', 'dp')), may hold values from 0 to 63, all different within a row; in each aligned block of 128 rows (0 to 127, 128 to 255, ...) at most 17 rows name the same one
- route_probs: bfloat16 [32768, 8], P(('expert', 'dp')), may hold values from 0.049804688 to 0.5
- w_gate_up: bfloat16 [64, 2048, 768], P('expert'), may hold values from -0.125 to 0.125
- w_down: bfloat16 [64, 2048, 384], P('expert'), may hold values from -0.3125 to 0.3125
Outputs:
- token_grad: bfloat16 [32768, 2048], P(('expert', 'dp'))
- prob_grad: bfloat16 [32768, 8], P(('expert', 'dp'))
- grad_gate_up: float32 [64, 2048, 768], P('expert', 'dp')
- grad_down: float32 [64, 2048, 384], P('expert', 'dp')
The draws below stay inside these ranges and needn't reach their ends.
Inputs may be any that keep to these rules, and one draw needn't show every extreme that they name: `expert_ids`: among the 128 tokens of one device (aligned blocks of rows) no expert is named by more than 17 tokens, a bound that some block reaches; a token names 8 different experts.
All inputs are finite; a program needn't handle non-finite values.
Results may differ from the reference program's by a relative error of at most 0.014.
Values may be sent and summed in bfloat16 or wider, within the bound.
A program may use at most 128 MiB of HBM per device.

```python
import math
import jax
import jax.numpy as jnp
import numpy as np
from jax import lax

D = 2048
FF = 384
TOP = 8
TOK_DEV = 128
EXPERTS = 64
CAP = 17
TOKENS = 32768


def shard_levels(rng, dims, split, low, high):
    loudness = 1.0
    for axis_at, parts in split:
        steps = jax.random.uniform(jax.random.fold_in(jax.random.fold_in(rng, 6), axis_at), (parts,), jnp.float32, low / len(split), high / len(split))
        loudness = loudness * jnp.repeat(jnp.exp(steps), dims[axis_at] // parts).reshape((-1,) + (1,) * (len(dims) - 1 - axis_at))
    return loudness


def assign_block(own_key, own, number, rows, count, top, most, slope):
    sequence = jax.random.permutation(own_key, count)
    packed, ordinary = portions_of(count, rows * top, most, slope, True), portions_of(count, rows * top, most, slope, False)
    places = jnp.arange(count)

    def named(lengths, offset_by):
        used = int((lengths > 0).sum())
        fixed = max(1, used // 4)
        moved = fixed + (places - fixed + offset_by * (used - fixed)) % max(1, count - fixed)
        return jnp.zeros((count,), jnp.int32).at[sequence[jnp.where(places < fixed, places, moved)]].set(jnp.asarray(lengths, jnp.int32))

    lengths = jnp.where(number % 4 == 0, named(packed, number // 4), named(ordinary, number - number // 4 - 1))
    mixed = jax.random.permutation(jax.random.fold_in(own, 3), count)
    giver, sink = mixed[0:count // 2 * 2:2], mixed[1:count // 2 * 2:2]
    room = jnp.minimum(lengths[giver] - 1, most - lengths[sink]) // 2
    room = jnp.where((giver == sequence[0]) | (sink == sequence[0]) | (lengths[sink] == 0), 0, jnp.maximum(room, 0))
    moved = jax.random.randint(jax.random.fold_in(own, 4), (count // 2,), 0, 1 << 20) % (room + 1)
    lengths = lengths.at[giver].add(-moved).at[sink].add(moved)
    items = jnp.searchsorted(jnp.cumsum(lengths), jnp.arange(rows * top), side="right").astype(jnp.int32)
    listing = items.reshape(top, rows).T
    listing = listing[jax.random.permutation(jax.random.fold_in(own, 1), rows)]
    offset_by = jax.random.randint(jax.random.fold_in(own, 2), (rows, 1), 0, top)
    return jnp.take_along_axis(listing, (jnp.arange(top)[None, :] + offset_by) % top, axis=1)


def portions_of(number_of, total, limit, lean, full):
    weights = [(1 << 20) // math.isqrt(standing ** lean) + 1 for standing in range(1, number_of + 1)]
    largest = limit if full else min(limit, max(-(-total // number_of), total * weights[0] // sum(weights)))
    least = 1 if total - largest >= number_of - 1 else 0
    counts, surplus = [largest] + [least] * (number_of - 1), total - largest - least * (number_of - 1)
    while surplus > 0:
        movable = [i for i in range(1, number_of) if counts[i] < largest] or [i for i in range(1, number_of) if counts[i] < limit]
        mass, remaining = sum([weights[i] for i in movable]), surplus
        for i in movable:
            addition = min(limit - counts[i], max(1, remaining * weights[i] // mass), surplus)
            counts[i] = counts[i] + addition
            surplus = surplus - addition
    return np.array(counts)


def normal_values(key, extent, width, most, pieces=(), held_as=jnp.bfloat16):
    loudness = shard_levels(key, extent, pieces, -0.22, 0.18) if pieces else 1.0
    array = jax.random.normal(key, extent, jnp.float32) * width * loudness
    return jnp.minimum(jnp.maximum(array, -most), most).astype(held_as)


def setup_inputs(seed: int = 0) -> dict:
    splits = jax.random.split(jax.random.key(seed), 7)
    tokens = normal_values(splits[0], (TOKENS, D), 1.0, 6.0, ((0, 256),))
    out_grad = normal_values(splits[1], (TOKENS, D), 1.0, 6.0, ((0, 256),))
    expert_ids_keys = jax.random.split(jax.random.fold_in(splits[2], 1), TOKENS // TOK_DEV)
    expert_ids_turns = jax.random.permutation(jax.random.fold_in(splits[2], 3), TOKENS // TOK_DEV)
    expert_ids = jax.vmap(lambda own, number: assign_block(jax.random.fold_in(splits[2], 2), own, number, TOK_DEV, EXPERTS, TOP, CAP, 2))(expert_ids_keys, expert_ids_turns).reshape((TOKENS, TOP))
    route_probs = jnp.clip(0.049804688 + 0.4501953 * jax.random.uniform(splits[3], (TOKENS, TOP), jnp.float32) ** shard_levels(splits[3], (TOKENS, TOP), ((0, 256),), -0.2, 0.2), 0.049804688, 0.5).astype(jnp.bfloat16)
    w_gate_up = normal_values(splits[4], (EXPERTS, D, 2 * FF), D ** -0.5, 0.125, ((0, 64),))
    w_down = normal_values(splits[5], (EXPERTS, D, FF), FF ** -0.5, 0.3125, ((0, 64),))
    return dict(tokens=tokens, out_grad=out_grad, expert_ids=expert_ids, route_probs=route_probs, w_gate_up=w_gate_up, w_down=w_down)


def slot_ranks(row_ids):
    onehot = (row_ids[:, None] == jnp.arange(EXPERTS, dtype=jnp.int32)[None, :]).astype(jnp.int32)
    return jnp.sum((jnp.cumsum(onehot, axis=0) - 1) * onehot, axis=1).astype(jnp.int32)


def reference(tokens, out_grad, expert_ids, route_probs, w_gate_up, w_down):
    block_count = TOKENS // TOK_DEV
    per_block = TOK_DEV * TOP
    flat_ids = expert_ids.reshape(block_count, per_block).astype(jnp.int32)
    ranks_all = lax.map(slot_ranks, flat_ids)
    block_index = jnp.broadcast_to(jnp.arange(block_count, dtype=jnp.int32)[:, None], (block_count, per_block))
    route_number = block_index * per_block + jnp.arange(per_block, dtype=jnp.int32)[None, :] + 1
    table = jnp.zeros((block_count, EXPERTS, CAP), jnp.int32).at[block_index, flat_ids, ranks_all].set(route_number)
    table = jnp.transpose(table, (1, 0, 2)).reshape(EXPERTS, block_count * CAP)
    flat_probs = route_probs.reshape(TOKENS * TOP)
    zero_bf = jnp.zeros((), jnp.bfloat16)

    def one_expert(carry, inputs):
        grad_sum, prob_sum = carry
        entry, weight_gu, weight_dn = inputs
        live_mask = entry > 0
        route_pick = jnp.maximum(entry - 1, 0)
        token_pick = route_pick // TOP
        x_in = jnp.where(live_mask[:, None], tokens[token_pick], zero_bf)
        dy_in = jnp.where(live_mask[:, None], out_grad[token_pick], zero_bf)
        p_in = jnp.where(live_mask, flat_probs[route_pick], zero_bf)
        gate_up = jnp.dot(x_in, weight_gu, preferred_element_type=jnp.float32)
        gate_val = gate_up[:, :FF]
        up_val = gate_up[:, FF:]
        sigmoid_gate = jax.nn.sigmoid(gate_val)
        silu_gate = gate_val * sigmoid_gate
        hidden_act = (silu_gate * up_val).astype(jnp.bfloat16)
        expert_out = lax.dot_general(hidden_act, weight_dn, (((1,), (1,)), ((), ())), preferred_element_type=jnp.float32)
        prob_slot = jnp.sum(dy_in.astype(jnp.float32) * expert_out, axis=1).astype(jnp.bfloat16)
        scaled_grad = (p_in.astype(jnp.float32)[:, None] * dy_in.astype(jnp.float32)).astype(jnp.bfloat16)
        hidden_grad = jnp.dot(scaled_grad, weight_dn, preferred_element_type=jnp.float32)
        gate_grad = hidden_grad * up_val * sigmoid_gate * (1.0 + gate_val * (1.0 - sigmoid_gate))
        up_grad = hidden_grad * silu_gate
        gate_up_grad = jnp.concatenate([gate_grad, up_grad], axis=1).astype(jnp.bfloat16)
        route_grad = lax.dot_general(gate_up_grad, weight_gu, (((1,), (1,)), ((), ())), preferred_element_type=jnp.float32).astype(jnp.bfloat16)
        grad_sum = grad_sum.at[token_pick].add(jnp.where(live_mask[:, None], route_grad.astype(jnp.float32), jnp.float32(0.0)))
        prob_sum = prob_sum.at[route_pick].add(jnp.where(live_mask, prob_slot.astype(jnp.float32), jnp.float32(0.0)))
        weight_gu_grad = lax.dot_general(x_in, gate_up_grad, (((0,), (0,)), ((), ())), preferred_element_type=jnp.float32)
        weight_dn_grad = lax.dot_general(scaled_grad, hidden_act, (((0,), (0,)), ((), ())), preferred_element_type=jnp.float32)
        return (grad_sum, prob_sum), (weight_gu_grad, weight_dn_grad)

    start = (jnp.zeros((TOKENS, D), jnp.float32), jnp.zeros((TOKENS * TOP,), jnp.float32))
    (grad_sum, prob_sum), (grad_gate_up, grad_down) = lax.scan(one_expert, start, (table, w_gate_up, w_down))
    token_grad = grad_sum.astype(jnp.bfloat16)
    prob_grad = prob_sum.reshape(TOKENS, TOP).astype(jnp.bfloat16)
    return (token_grad, prob_grad, grad_gate_up, grad_down)
```

```python
import functools

import jax
import jax.numpy as jnp
from jax import lax
from jax.experimental import pallas as pl
from jax.experimental.pallas import tpu as pltpu
from jax.sharding import PartitionSpec as P

MESH = pl.DeviceIdType.MESH
BF = jnp.bfloat16
F32 = jnp.float32

NZ = 8
COL = 8
TOK = 128
D = 2048
FF = 384
SLOT = 16
MAIN = COL * SLOT
ROWS = NZ * MAIN + COL * NZ
BACK = D + 128
OVB = D // 2 + 128
CW = 256


def iota(shape, dim):
    return lax.broadcasted_iota(jnp.int32, shape, dim)


def dot(a, b):
    return jnp.dot(a, b, preferred_element_type=F32)


def dot_nt(a, b):
    return lax.dot_general(a, b, (((1,), (1,)), ((), ())), preferred_element_type=F32)


def dot_tn(a, b):
    return lax.dot_general(a, b, (((0,), (0,)), ((), ())), preferred_element_type=F32)


def tile(n, width=CW):
    return pl.ds(pl.multiple_of(n * width, width), width)


def rows16(start, count):
    return pl.ds(pl.multiple_of(start, 16), count)


def mask(cond, dtype=BF):
    return jnp.where(cond, 1.0, 0.0).astype(dtype)


def kernel(
    tok_ref, dy_ref, ids_ref, probs_ref, wgu_hbm, wdn_hbm,
    out_tok, out_prob, out_gu, out_dn,
    wgu, wdn, meta_own, meta_all, sel, sel_t, sov_t, blk, sendbuf, ovf32, ovsend, ovrecv,
    xs, gu, hg, hbuf, dgu, retbuf, retrecv, retov, retovr, rovf, tf, rsr, gsend, grecv,
    w_sem, meta_s, meta_r, ag_s, ag_r, d_s, d_r, ov_s, ov_r, r_s, r_r, ro_s, ro_r, rs_s, rs_r, g_s, g_r,
):
    e = lax.axis_index("expert")
    x = lax.axis_index("dp")
    y, z, c = e // 16, (e // 2) % 8, e % 2
    s = y * 2 + c
    sgn = 1 - 2 * c
    expert_lane = z * 8 + s

    def zdev(k):
        return ((y * 8 + (z + k + 8) % 8) * 2 + c, x)

    def coldev(t):
        return (((t // 2) * 8 + z) * 2 + t % 2, x)

    def xdev(k):
        return (e, (x + k + 4) % 4)

    def remote(src, dst, ss, rs, dev):
        return pltpu.make_async_remote_copy(
            src_ref=src, dst_ref=dst, send_sem=ss, recv_sem=rs, device_id=dev, device_id_type=MESH
        )

    def loop(lo, hi, fn):
        def step(i, carry):
            fn(i)
            return carry

        lax.fori_loop(lo, hi, step, 0)

    def meta_copy(i):
        return remote(
            meta_own.at[(z + i) % 8], meta_all.at[i], meta_s.at[i], meta_r.at[i], zdev(i)
        )

    def ag_copy(src, pos, p, k):
        return remote(src, blk.at[pos - 1, p], ag_s.at[pos - 1, p], ag_r.at[pos - 1, p], zdev(k))

    def row_copy(pos, p, i):
        t = (s + i) % 8
        return remote(
            sendbuf.at[pos, p, rows16(t * SLOT, SLOT)],
            xs.at[p, rows16(pos * MAIN + s * SLOT, SLOT)],
            d_s.at[pos * 2 + p, i],
            d_r.at[pos * 2 + p, i],
            coldev(t),
        )

    def over_copy(i):
        t = (s + i) % 8
        return remote(
            ovsend.at[rows16(t * 16, 16)], ovrecv.at[rows16(s * 16, 16)], ov_s.at[i], ov_r.at[i], coldev(t)
        )

    def back_copy(pos, i):
        t = (s + i) % 8
        return remote(
            retbuf.at[rows16(pos * MAIN + t * SLOT, SLOT)],
            retrecv.at[pos, rows16(s * SLOT, SLOT)],
            r_s.at[pos, i],
            r_r.at[pos, i],
            coldev(t),
        )

    def back_over_copy(i):
        t = (s + i) % 8
        return remote(
            retov.at[rows16(t * 16, 16)], retovr.at[rows16(s * 16, 16)], ro_s.at[i], ro_r.at[i], coldev(t)
        )

    def sum_copy(pos, piece, k):
        return remote(
            retbuf.at[rows16(pos * MAIN + piece * 64, 64)],
            rsr.at[pos - 1, rows16(piece * 64, 64)],
            rs_s.at[pos - 1, piece],
            rs_r.at[pos - 1, piece],
            zdev(k),
        )

    def grad_copy(slot, k):
        return remote(
            gsend.at[slot % 2], grecv.at[slot], g_s.at[slot], g_r.at[slot], xdev(k)
        )

    barrier = pltpu.get_barrier_semaphore()
    for i in range(1, 8):
        pl.semaphore_signal(barrier, inc=1, device_id=zdev(i), device_id_type=MESH)
        pl.semaphore_signal(barrier, inc=1, device_id=coldev((s + i) % 8), device_id_type=MESH)
    for k in (-1, 1):
        pl.semaphore_signal(barrier, inc=1, device_id=xdev(k), device_id_type=MESH)
    pl.semaphore_wait(barrier, 16)

    for p, ref in ((0, tok_ref), (1, dy_ref)):
        ag_copy(ref, 1, p, sgn).start()
        ag_copy(ref, 2, p, -sgn).start()
    w_gu_copy = pltpu.make_async_copy(wgu_hbm, wgu, w_sem.at[0])
    w_dn_copy = pltpu.make_async_copy(wdn_hbm, wdn, w_sem.at[1])
    w_gu_copy.start()
    w_dn_copy.start()

    def by_z(ids):
        return ((ids // 2) % 8) * 8 + (ids // 16) * 2 + ids % 2

    eye8 = mask(iota((8, 8), 0) == iota((8, 8), 1))
    ids_t = dot_nt(eye8, by_z(ids_ref[...]).astype(F32).astype(BF))
    probs_t = dot_nt(eye8, probs_ref[...])
    lane_of = iota((64, TOK), 0).astype(F32)
    named = jnp.zeros((64, TOK), F32)
    weight = jnp.zeros((64, TOK), F32)
    for k in range(8):
        hit = ids_t[k : k + 1, :] == lane_of
        named += jnp.where(hit, 1.0, 0.0)
        weight += jnp.where(hit, probs_t[k : k + 1, :], 0.0)
    before = mask(iota((TOK, TOK), 0) < iota((TOK, TOK), 1))
    rank = jnp.where(named > 0.0, dot(named.astype(BF), before), -1.0)
    for k in range(NZ):
        meta_own[k, 0:8, :] = rank[k * 8 : k * 8 + 8]
        meta_own[k, 8:16, :] = weight[k * 8 : k * 8 + 8]
    loop(1, 8, lambda i: meta_copy(i).start())

    def build(pos, info):
        ranks, weights = info[0:8], info[8:16]

        def spread(a, n):
            return jnp.concatenate([jnp.broadcast_to(a[k : k + 1], (n, TOK)) for k in range(8)], axis=0)

        hit = spread(ranks, SLOT) == (iota((MAIN, TOK), 0) % SLOT).astype(F32)
        over = ranks == float(SLOT)
        none = jnp.zeros((8, TOK), F32)
        one = jnp.where(hit, 1.0, 0.0)
        sel[0, pos, 0:MAIN, :] = one.astype(BF)
        sel[0, pos, MAIN : MAIN + 16, :] = jnp.concatenate([jnp.where(over, 1.0, 0.0), none], axis=0).astype(BF)
        sel[1, pos, 0:MAIN, :] = jnp.where(hit, spread(weights, SLOT), 0.0).astype(BF)
        sel[1, pos, MAIN : MAIN + 16, :] = jnp.concatenate([jnp.where(over, weights, 0.0), none], axis=0).astype(BF)
        sel_t[pos] = one.T.astype(BF)
        mine = (spread(ranks, 8) == float(SLOT)) & (iota((64, TOK), 0) % 8 == pos)
        wide = jnp.concatenate([jnp.where(mine, 1.0, 0.0), jnp.zeros((64, TOK), F32)], axis=0)
        sov_t[pos] = wide.T.astype(BF)

    def pick(pos, p, ref):
        def column(n):
            got = dot(sel[p, pos], ref[:, tile(n)])
            sendbuf[pos, p, :, tile(n)] = got[:MAIN].astype(BF)
            ovf32[p, pl.ds(pl.multiple_of(pos * 8, 8), 8), tile(n)] = got[MAIN : MAIN + 8]

        loop(0, D // CW, column)
        loop(1, 8, lambda i: row_copy(pos, p, i).start())
        xs[p, rows16(pos * MAIN + s * SLOT, SLOT), :] = sendbuf[pos, p, rows16(s * SLOT, SLOT), :]

    def await_rows(pos):
        loop(1, 8, lambda i: row_copy(pos, 0, i).wait_recv())
        loop(1, 8, lambda i: row_copy(pos, 1, i).wait_recv())

    def expert(row0, count):
        rows = rows16(row0, count)

        def first(n):
            gu[0:count, tile(n)] = dot(xs[0, rows, :], wgu[:, tile(n)])

        loop(0, 2 * FF // CW, first)

        def second(n):
            hg[0:count, tile(n, 128)] = dot(xs[1, rows, :], wdn[:, tile(n, 128)])

        loop(0, FF // 128, second)

        def middle(n):
            part, whole = rows16(n * 32, 32), rows16(row0 + n * 32, 32)
            gate, up, grad = gu[part, 0:FF], gu[part, FF : 2 * FF], hg[part, :]
            sig = jax.nn.sigmoid(gate)
            silu = gate * sig
            act = (silu * up).astype(BF)
            hbuf[whole, :] = act
            dgu[whole, 0:FF] = (grad * up * sig * (1.0 + gate * (1.0 - sig))).astype(BF)
            dgu[whole, FF : 2 * FF] = (grad * silu).astype(BF)
            router = jnp.sum(grad * act.astype(F32), axis=1, keepdims=True)
            retbuf[whole, D:BACK] = jnp.where(iota((32, 128), 1) == expert_lane, router, 0.0).astype(BF)

        loop(0, count // 32, middle)

        def last(n):
            retbuf[rows, tile(n)] = dot_nt(dgu[rows, :], wgu[tile(n), :]).astype(BF)

        loop(0, D // CW, last)

    build(0, meta_own[z])
    pick(0, 0, tok_ref)
    pick(0, 1, dy_ref)
    w_gu_copy.wait()
    w_dn_copy.wait()

    r128, c64 = iota((128, 64), 0), iota((128, 64), 1)
    r64, c128 = iota((64, 128), 0), iota((64, 128), 1)

    def turn(d):
        odd, even = 2 * d - 1, 2 * d
        up_at, down_at = (8 + sgn * d) % 8, (8 - sgn * d) % 8
        meta_copy(up_at).wait_recv()
        build(odd, meta_all[up_at])

        @pl.when(d < 4)
        def _():
            meta_copy(down_at).wait_recv()
            build(even, meta_all[down_at])

        def piece(p):
            ag_copy(tok_ref, odd, p, sgn).wait_recv()

            @pl.when(d < 4)
            def _():
                ag_copy(blk.at[odd - 1, p], odd + 2, p, sgn).start()

            pick(odd, p, blk.at[odd - 1, p])

            @pl.when(d < 4)
            def _():
                ag_copy(tok_ref, even, p, -sgn).wait_recv()

                @pl.when(d < 3)
                def _():
                    ag_copy(blk.at[even - 1, p], even + 2, p, -sgn).start()

                pick(even, p, blk.at[even - 1, p])

        loop(0, 2, piece)

        @pl.when(d == 4)
        def _():
            where_of = c64 == (r128 % 8) * 8 + r128 // 16
            first, second = mask((r128 % 16 < 8) & where_of), mask((r128 % 16 >= 8) & where_of)

            def column(n):
                a, b = ovf32[0, :, tile(n)].astype(BF), ovf32[1, :, tile(n)].astype(BF)
                ovsend[:, tile(n)] = (dot(first, a) + dot(second, b)).astype(BF)

            loop(0, D // CW, column)
            loop(1, 8, lambda i: over_copy(i).start())
            ovrecv[rows16(s * 16, 16), :] = ovsend[rows16(s * 16, 16), :]

        @pl.when(d >= 2)
        def _():
            await_rows(2 * d - 4)
            await_rows(2 * d - 3)
            expert((2 * d - 4) * MAIN, 2 * MAIN)

    loop(1, 5, turn)

    await_rows(6)
    await_rows(7)
    loop(1, 8, lambda i: over_copy(i).wait_recv())
    take_lo = mask(c128 == (r64 // 8) * 16 + r64 % 8)
    take_hi = mask(c128 == (r64 // 8) * 16 + 8 + r64 % 8)

    def unpack(n):
        got = ovrecv[:, tile(n)]
        xs[0, NZ * MAIN : ROWS, tile(n)] = dot(take_lo, got).astype(BF)
        xs[1, NZ * MAIN : ROWS, tile(n)] = dot(take_hi, got).astype(BF)

    loop(0, D // CW, unpack)
    expert(6 * MAIN, ROWS - 6 * MAIN)

    put_lo = mask((r128 % 16 < 8) & (c64 == (r128 // 16) * 8 + r128 % 16))
    put_hi = mask((r128 % 16 >= 8) & (c64 == (r128 // 16) * 8 + r128 % 16 - 8))
    over_rows = pl.ds(NZ * MAIN, COL * NZ)

    def pack(n):
        lo, hi = retbuf[over_rows, tile(n)], retbuf[over_rows, tile(n + 4)]
        retov[:, tile(n)] = (dot(put_lo, lo) + dot(put_hi, hi)).astype(BF)

    loop(0, D // 2 // CW, pack)
    retov[:, D // 2 : OVB] = dot(put_lo, retbuf[over_rows, D:BACK]).astype(BF)
    loop(1, 8, lambda i: back_over_copy(i).start())
    retovr[rows16(s * 16, 16), :] = retov[rows16(s * 16, 16), :]

    def send_back(k):
        pos = NZ - 1 - k
        loop(1, 8, lambda i: back_copy(pos, i).start())
        retrecv[pos, rows16(s * SLOT, SLOT), :] = retbuf[rows16(pos * MAIN + s * SLOT, SLOT), :]

    loop(0, NZ, send_back)

    def weight_grad(j, emit):
        def half(m):
            cols = pl.ds(pl.multiple_of(j * 512 + m * CW, CW), CW)
            emit(m, dot_tn(xs[0, :, cols], dgu[...]), dot_tn(xs[1, :, cols], hbuf[...]))

        loop(0, 2, half)

    def emit_send(slot):
        def emit(m, a, b):
            gsend[slot, tile(m), 0 : 2 * FF] = a.astype(BF)
            gsend[slot, tile(m), 2 * FF :] = b.astype(BF)

        return emit

    weight_grad((x + 2) % 4, emit_send(0))
    grad_copy(0, sgn).start()
    weight_grad((x - sgn + 4) % 4, emit_send(1))
    grad_copy(1, -sgn).start()

    def emit_own(m, a, b):
        out_gu[tile(m), :] = a
        out_dn[tile(m), :] = b

    weight_grad(x, emit_own)

    loop(1, 8, lambda i: back_over_copy(i).wait_recv())

    def unpack_back(n):
        got = retovr[:, tile(n)]
        rovf[0:64, tile(n)] = dot(take_lo, got).astype(BF)
        rovf[0:64, tile(n + 4)] = dot(take_hi, got).astype(BF)

    loop(0, D // 2 // CW, unpack_back)
    rovf[0:64, D:BACK] = dot(take_lo, retovr[:, D // 2 : OVB]).astype(BF)
    rovf[64:128, :] = jnp.zeros((64, BACK), BF)

    def combine(pos):
        loop(1, 8, lambda i: back_copy(pos, i).wait_recv())

        def column(n):
            tf[:, tile(n)] = dot(sel_t[pos], retrecv[pos, :, tile(n)]) + dot(sov_t[pos], rovf[:, tile(n)])

        loop(0, D // CW, column)
        tf[:, D:BACK] = dot(sel_t[pos], retrecv[pos, :, D:BACK]) + dot(sov_t[pos], rovf[:, D:BACK])

    def pass_on(pos, k, has_more):
        combine(pos)
        loop(1, 8, lambda i: back_copy(pos, i).wait_send())

        def piece(h):
            @pl.when(has_more)
            def _():
                sum_copy(pos + 2, h, k).wait_recv()

                def part(n):
                    at = rows16(h * 64 + n * 16, 16)
                    total = tf[at, :] + rsr[pos + 1, at, :].astype(F32)
                    retbuf[rows16(pos * MAIN + h * 64 + n * 16, 16), :] = total.astype(BF)

                loop(0, 4, part)

            @pl.when(jnp.logical_not(has_more))
            def _():
                def part(n):
                    at = rows16(h * 64 + n * 16, 16)
                    retbuf[rows16(pos * MAIN + h * 64 + n * 16, 16), :] = tf[at, :].astype(BF)

                loop(0, 4, part)

            sum_copy(pos, h, k).start()

        loop(0, 2, piece)

    def back_turn(k):
        d = 4 - k
        pass_on(2 * d - 1, -sgn, d < 4)

        @pl.when(d < 4)
        def _():
            pass_on(2 * d, sgn, d < 3)

        @pl.when(d == 2)
        def _():
            grad_copy(0, sgn).wait()

            def emit(m, a, b):
                got = grecv[0, tile(m), :].astype(F32)
                gsend[0, tile(m), 0 : 2 * FF] = (a + got[:, 0 : 2 * FF]).astype(BF)
                gsend[0, tile(m), 2 * FF :] = (b + got[:, 2 * FF :]).astype(BF)

            weight_grad((x + sgn + 4) % 4, emit)
            grad_copy(2, sgn).start()

    loop(0, 4, back_turn)

    combine(0)
    for pos in (1, 2):
        for h in (0, 1):
            sum_copy(pos, h, sgn).wait_recv()

    def finish(n):
        at = rows16(n * 16, 16)
        total = tf[at, :] + rsr[0, at, :].astype(F32) + rsr[1, at, :].astype(F32)
        out_tok[at, :] = total[:, 0:D].astype(BF)
        tf[at, D:BACK] = total[:, D:BACK]

    loop(0, TOK // 16, finish)
    router = tf[:, D:BACK]
    ids = by_z(ids_ref[...])
    found = jnp.zeros((TOK, 8), F32)
    for k in range(8):
        hit = ids[:, k : k + 1] == iota((TOK, 128), 1)
        value = jnp.sum(jnp.where(hit, router, 0.0), axis=1, keepdims=True)
        found = jnp.where(iota((TOK, 8), 1) == k, value, found)
    out_prob[...] = (found / probs_ref[...].astype(F32)).astype(BF)

    grad_copy(1, -sgn).wait()
    grad_copy(2, sgn).wait()

    def add_grads(n):
        at = rows16(n * 32, 32)
        more = grecv[1, at, :].astype(F32) + grecv[2, at, :].astype(F32)
        out_gu[at, :] = out_gu[at, :] + more[:, 0 : 2 * FF]
        out_dn[at, :] = out_dn[at, :] + more[:, 2 * FF :]

    loop(0, 512 // 32, add_grads)

    loop(1, 8, lambda i: meta_copy(i).wait_send())
    loop(1, 8, lambda i: over_copy(i).wait_send())
    loop(1, 8, lambda i: back_over_copy(i).wait_send())
    loop(1, 8, lambda i: back_copy(0, i).wait_send())

    def drain(pos):
        loop(1, 8, lambda i: row_copy(pos, 0, i).wait_send())
        loop(1, 8, lambda i: row_copy(pos, 1, i).wait_send())

    loop(0, NZ, drain)

    def drain_ring(pos):
        def piece(h):
            ag_copy(tok_ref, pos, h, sgn).wait_send()
            sum_copy(pos, h, sgn).wait_send()

        loop(0, 2, piece)

    loop(1, 8, drain_ring)


def on_device(tokens, out_grad, expert_ids, route_probs, w_gate_up, w_down):
    vm, dma = pltpu.VMEM, pltpu.SemaphoreType.DMA
    inside = pl.BlockSpec(memory_space=pltpu.VMEM)
    token_grad, prob_grad, grad_gu, grad_dn = pl.pallas_call(
        kernel,
        out_shape=(
            jax.ShapeDtypeStruct((TOK, D), BF),
            jax.ShapeDtypeStruct((TOK, 8), BF),
            jax.ShapeDtypeStruct((512, 2 * FF), F32),
            jax.ShapeDtypeStruct((512, FF), F32),
        ),
        in_specs=[inside] * 4 + [pl.BlockSpec(memory_space=pl.ANY)] * 2,
        out_specs=(inside,) * 4,
        scratch_shapes=[
            vm((D, 2 * FF), BF),
            vm((D, FF), BF),
            vm((NZ, 16, TOK), F32),
            vm((NZ, 16, TOK), F32),
            vm((2, NZ, MAIN + 16, TOK), BF),
            vm((NZ, TOK, MAIN), BF),
            vm((NZ, TOK, 128), BF),
            vm((NZ - 1, 2, TOK, D), BF),
            vm((NZ, 2, MAIN, D), BF),
            vm((2, 64, D), F32),
            vm((128, D), BF),
            vm((128, D), BF),
            vm((2, ROWS, D), BF),
            vm((320, 2 * FF), F32),
            vm((320, FF), F32),
            vm((ROWS, FF), BF),
            vm((ROWS, 2 * FF), BF),
            vm((ROWS, BACK), BF),
            vm((NZ, MAIN, BACK), BF),
            vm((128, OVB), BF),
            vm((128, OVB), BF),
            vm((128, BACK), BF),
            vm((TOK, BACK), F32),
            vm((NZ - 1, TOK, BACK), BF),
            vm((2, 512, 3 * FF), BF),
            vm((3, 512, 3 * FF), BF),
            dma((2,)),
            dma((8,)), dma((8,)),
            dma((7, 2)), dma((7, 2)),
            dma((16, 8)), dma((16, 8)),
            dma((8,)), dma((8,)),
            dma((8, 8)), dma((8, 8)),
            dma((8,)), dma((8,)),
            dma((7, 2)), dma((7, 2)),
            dma((3,)), dma((3,)),
        ],
        compiler_params=pltpu.CompilerParams(
            collective_id=0, has_side_effects=True, vmem_limit_bytes=62 * 2**20
        ),
        cost_estimate=pl.CostEstimate(flops=15 * 10**9, bytes_accessed=10**7, transcendentals=10**6),
        name="routed_backward",
    )(tokens, out_grad, expert_ids, route_probs, w_gate_up[0], w_down[0])
    return token_grad, prob_grad, grad_gu[None], grad_dn[None]


def solution(mesh):
    in_specs = (
        P(("expert", "dp"), None),
        P(("expert", "dp"), None),
        P(("expert", "dp"), None),
        P(("expert", "dp"), None),
        P("expert", None, None),
        P("expert", None, None),
    )
    out_specs = (
        P(("expert", "dp"), None),
        P(("expert", "dp"), None),
        P("expert", "dp", None),
        P("expert", "dp", None),
    )
    return jax.shard_map(
        on_device, mesh=mesh, in_specs=in_specs, out_specs=out_specs, check_vma=False
    )
```

```python
import functools

import jax
import jax.numpy as jnp
from jax import lax
from jax.experimental import pallas as pl
from jax.experimental.pallas import tpu as pltpu
from jax.sharding import PartitionSpec as P

MESH = pl.DeviceIdType.MESH
BF = jnp.bfloat16
F32 = jnp.float32

NZ = 8
COL = 8
TOK = 128
D = 2048
FF = 384
SLOT = 16
MAIN = COL * SLOT
ROWS = NZ * MAIN + COL * NZ
BACK = D + 128
OVB = D // 2 + 128
OVER = (NZ - 1) * MAIN
CW = 256


def iota(shape, dim):
    return lax.broadcasted_iota(jnp.int32, shape, dim)


def dot(a, b):
    return jnp.dot(a, b, preferred_element_type=F32)


def dot_nt(a, b):
    return lax.dot_general(a, b, (((1,), (1,)), ((), ())), preferred_element_type=F32)


def dot_tn(a, b):
    return lax.dot_general(a, b, (((0,), (0,)), ((), ())), preferred_element_type=F32)


def tile(n, width=CW):
    return pl.ds(pl.multiple_of(n * width, width), width)


def rows16(start, count):
    return pl.ds(pl.multiple_of(start, 16), count)


def mask(cond, dtype=BF):
    return jnp.where(cond, 1.0, 0.0).astype(dtype)


def kernel(
    tok_ref, dy_ref, ids_ref, probs_ref, wgu_hbm, wdn_hbm,
    out_tok, out_prob, out_gu, out_dn,
    wgu, wdn, meta_own, meta_all, far, far_in, sel, sel_t, sov_t, blk, sendbuf, ovf32, ovsend, ovrecv,
    xs, gu, hg, hbuf, dgu, retbuf, retrecv, retov, retovr, rovf, tf, rsr, gsend, grecv,
    w_sem, far_sem, meta_s, meta_r, ag_s, ag_r, d_s, d_r, ov_s, ov_r, r_s, r_r, ro_s, ro_r, rs_s, rs_r, g_s, g_r,
):
    e = lax.axis_index("expert")
    x = lax.axis_index("dp")
    y, z, c = e // 16, (e // 2) % 8, e % 2
    s = y * 2 + c
    sgn = 1 - 2 * c
    expert_lane = z * 8 + s

    def zdev(k):
        return ((y * 8 + (z + k + 8) % 8) * 2 + c, x)

    def coldev(t):
        return (((t // 2) * 8 + z) * 2 + t % 2, x)

    def xdev(k):
        return (e, (x + k + 4) % 4)

    def remote(src, dst, ss, rs, dev):
        return pltpu.make_async_remote_copy(
            src_ref=src, dst_ref=dst, send_sem=ss, recv_sem=rs, device_id=dev, device_id_type=MESH
        )

    def base(pos):
        return pos * MAIN + (pos // (NZ - 1)) * COL * NZ

    def loop(lo, hi, fn):
        def step(i, carry):
            fn(i)
            return carry

        lax.fori_loop(lo, hi, step, 0)

    def meta_copy(i):
        return remote(
            meta_own.at[(z + i) % 8], meta_all.at[i], meta_s.at[i], meta_r.at[i], zdev(i)
        )

    def ag_copy(src, pos, p, k):
        return remote(src, blk.at[pos - 1, p], ag_s.at[pos - 1, p], ag_r.at[pos - 1, p], zdev(k))

    def row_copy(pos, p, i):
        t = (s + i) % 8
        return remote(
            sendbuf.at[pos, p, rows16(t * SLOT, SLOT)],
            xs.at[p, rows16(base(pos) + s * SLOT, SLOT)],
            d_s.at[pos * 2 + p, i],
            d_r.at[pos * 2 + p, i],
            coldev(t),
        )

    def over_copy(i):
        t = (s + i) % 8
        return remote(
            ovsend.at[rows16(t * 16, 16)], ovrecv.at[rows16(s * 16, 16)], ov_s.at[i], ov_r.at[i], coldev(t)
        )

    def back_copy(pos, i):
        t = (s + i) % 8
        return remote(
            retbuf.at[rows16(base(pos) + t * SLOT, SLOT)],
            retrecv.at[pos, rows16(s * SLOT, SLOT)],
            r_s.at[pos, i],
            r_r.at[pos, i],
            coldev(t),
        )

    def back_over_copy(i):
        t = (s + i) % 8
        return remote(
            retov.at[rows16(t * 16, 16)], retovr.at[rows16(s * 16, 16)], ro_s.at[i], ro_r.at[i], coldev(t)
        )

    def sum_copy(pos, piece, k):
        return remote(
            retbuf.at[rows16(base(pos) + piece * 64, 64)],
            rsr.at[pos - 1, rows16(piece * 64, 64)],
            rs_s.at[pos - 1, piece],
            rs_r.at[pos - 1, piece],
            zdev(k),
        )

    def grad_copy(slot, half, k):
        return remote(
            gsend.at[slot % 2, tile(half)],
            grecv.at[slot, tile(half)],
            g_s.at[slot, half],
            g_r.at[slot, half],
            xdev(k),
        )

    def far_copy():
        return remote(far, far_in, far_sem.at[0], far_sem.at[1], zdev(4))

    w_gu_copy = pltpu.make_async_copy(wgu_hbm, wgu, w_sem.at[0])
    w_dn_copy = pltpu.make_async_copy(wdn_hbm, wdn, w_sem.at[1])
    w_gu_copy.start()
    w_dn_copy.start()

    barrier = pltpu.get_barrier_semaphore()
    for i in range(1, 8):
        pl.semaphore_signal(barrier, inc=1, device_id=zdev(i), device_id_type=MESH)
        pl.semaphore_signal(barrier, inc=1, device_id=coldev((s + i) % 8), device_id_type=MESH)
    for k in (-1, 1):
        pl.semaphore_signal(barrier, inc=1, device_id=xdev(k), device_id_type=MESH)
    def by_z(ids):
        return ((ids // 2) % 8) * 8 + (ids // 16) * 2 + ids % 2

    ids_t = by_z(ids_ref[...])
    probs_t = probs_ref[...].astype(F32)
    lane_of = iota((64, TOK), 0)
    named = jnp.zeros((64, TOK), F32)
    weight = jnp.zeros((64, TOK), F32)
    for k in range(8):
        hit = ids_t[k : k + 1, :] == lane_of
        named += jnp.where(hit, 1.0, 0.0)
        weight += jnp.where(hit, probs_t[k : k + 1, :], 0.0)
    before = mask(iota((TOK, TOK), 0) < iota((TOK, TOK), 1))
    rank = jnp.where(named > 0.0, dot(named.astype(BF), before), -1.0)
    for k in range(NZ):
        meta_own[k, 0:8, :] = rank[k * 8 : k * 8 + 8]
        meta_own[k, 8:16, :] = weight[k * 8 : k * 8 + 8]

    def build(pos, info):
        ranks, weights = info[0:8], info[8:16]

        def spread(a, n):
            return jnp.concatenate([jnp.broadcast_to(a[k : k + 1], (n, TOK)) for k in range(8)], axis=0)

        hit = spread(ranks, SLOT) == (iota((MAIN, TOK), 0) % SLOT).astype(F32)
        over = ranks == float(SLOT)
        none = jnp.zeros((8, TOK), F32)
        one = jnp.where(hit, 1.0, 0.0)
        sel[0, pos, 0:MAIN, :] = one.astype(BF)
        sel[0, pos, MAIN : MAIN + 16, :] = jnp.concatenate([jnp.where(over, 1.0, 0.0), none], axis=0).astype(BF)
        sel[1, pos, 0:MAIN, :] = jnp.where(hit, spread(weights, SLOT), 0.0).astype(BF)
        sel[1, pos, MAIN : MAIN + 16, :] = jnp.concatenate([jnp.where(over, weights, 0.0), none], axis=0).astype(BF)
        sel_t[pos] = one.T.astype(BF)
        mine = (spread(ranks, 8) == float(SLOT)) & (iota((64, TOK), 0) % 8 == pos)
        wide = jnp.concatenate([jnp.where(mine, 1.0, 0.0), jnp.zeros((64, TOK), F32)], axis=0)
        sov_t[pos] = wide.T.astype(BF)

    def pick(pos, p, ref):
        def column(n):
            got = dot(sel[p, pos], ref[:, tile(n)])
            sendbuf[pos, p, :, tile(n)] = got[:MAIN].astype(BF)
            ovf32[p, pl.ds(pl.multiple_of(pos * 8, 8), 8), tile(n)] = got[MAIN : MAIN + 8]

        loop(0, D // CW, column)

    def send(pos, p):
        loop(1, 8, lambda i: row_copy(pos, p, i).start())
        xs[p, rows16(base(pos) + s * SLOT, SLOT), :] = sendbuf[pos, p, rows16(s * SLOT, SLOT), :]

    def await_rows(pos):
        loop(1, 8, lambda i: row_copy(pos, 0, i).wait_recv())
        loop(1, 8, lambda i: row_copy(pos, 1, i).wait_recv())

    def expert(row0, count):
        rows = rows16(row0, count)

        def first(n):
            gu[0:count, tile(n)] = dot(xs[0, rows, :], wgu[:, tile(n)])

        loop(0, 2 * FF // CW, first)

        def second(n):
            hg[0:count, tile(n, 128)] = dot(xs[1, rows, :], wdn[:, tile(n, 128)])

        loop(0, FF // 128, second)

        def middle(n):
            part, whole = rows16(n * 32, 32), rows16(row0 + n * 32, 32)
            gate, up, grad = gu[part, 0:FF], gu[part, FF : 2 * FF], hg[part, :]
            sig = jax.nn.sigmoid(gate)
            silu = gate * sig
            act = (silu * up).astype(BF)
            hbuf[whole, :] = act
            dgu[whole, 0:FF] = (grad * up * sig * (1.0 + gate * (1.0 - sig))).astype(BF)
            dgu[whole, FF : 2 * FF] = (grad * silu).astype(BF)
            router = jnp.sum(grad * act.astype(F32), axis=1, keepdims=True)
            retbuf[whole, D:BACK] = jnp.where(iota((32, 128), 1) == expert_lane, router, 0.0).astype(BF)

        loop(0, count // 32, middle)

        def last(n):
            retbuf[rows, tile(n)] = dot_nt(dgu[rows, :], wgu[tile(n), :]).astype(BF)

        loop(0, D // CW, last)

    build(0, meta_own[z])
    pick(0, 0, tok_ref)
    pick(0, 1, dy_ref)
    opposite = meta_own[(z + 4) % 8]
    nobody = jnp.zeros((8, TOK), F32)
    far_one = jnp.concatenate([jnp.where(opposite[0:8] == float(SLOT), 1.0, 0.0), nobody], axis=0).astype(BF)
    far_weight = jnp.concatenate([nobody, jnp.where(opposite[0:8] == float(SLOT), opposite[8:16], 0.0)], axis=0).astype(BF)

    def far_rows(n):
        far[:, tile(n)] = (dot(far_one, tok_ref[:, tile(n)]) + dot(far_weight, dy_ref[:, tile(n)])).astype(BF)

    loop(0, D // CW, far_rows)

    pl.semaphore_wait(barrier, 16)

    ag_copy(tok_ref, 1, 0, sgn).start()
    ag_copy(tok_ref, 2, 0, -sgn).start()
    send(0, 0)
    loop(1, 8, lambda i: meta_copy(i).start())
    ag_copy(dy_ref, 1, 1, sgn).start()
    ag_copy(dy_ref, 2, 1, -sgn).start()
    send(0, 1)
    far_copy().start()
    w_gu_copy.wait()
    w_dn_copy.wait()

    r128, c64 = iota((128, 64), 0), iota((128, 64), 1)
    r64, c128 = iota((64, 128), 0), iota((64, 128), 1)

    def turn(d):
        odd, even = 2 * d - 1, 2 * d
        up_at, down_at = (8 + sgn * d) % 8, (8 - sgn * d) % 8
        meta_copy(up_at).wait_recv()
        build(odd, meta_all[up_at])

        @pl.when(d < 4)
        def _():
            meta_copy(down_at).wait_recv()
            build(even, meta_all[down_at])

        def piece(p):
            ag_copy(tok_ref, odd, p, sgn).wait_recv()

            @pl.when(d < 4)
            def _():
                ag_copy(blk.at[odd - 1, p], odd + 2, p, sgn).start()

            pick(odd, p, blk.at[odd - 1, p])
            send(odd, p)

            @pl.when(d < 4)
            def _():
                ag_copy(tok_ref, even, p, -sgn).wait_recv()

                @pl.when(d < 3)
                def _():
                    ag_copy(blk.at[even - 1, p], even + 2, p, -sgn).start()

                pick(even, p, blk.at[even - 1, p])
                send(even, p)

        loop(0, 2, piece)

        @pl.when(d == 3)
        def _():
            far_copy().wait_recv()
            ovf32[0, 56:64, :] = far_in[...].astype(F32)[0:8]
            ovf32[1, 56:64, :] = far_in[...].astype(F32)[8:16]
            where_of = c64 == (r128 % 8) * 8 + r128 // 16
            first, second = mask((r128 % 16 < 8) & where_of), mask((r128 % 16 >= 8) & where_of)

            def column(n):
                a, b = ovf32[0, :, tile(n)].astype(BF), ovf32[1, :, tile(n)].astype(BF)
                ovsend[:, tile(n)] = (dot(first, a) + dot(second, b)).astype(BF)

            loop(0, D // CW, column)
            loop(1, 8, lambda i: over_copy(i).start())
            ovrecv[rows16(s * 16, 16), :] = ovsend[rows16(s * 16, 16), :]

        @pl.when(d >= 2)
        def _():
            await_rows(2 * d - 4)
            await_rows(2 * d - 3)
            expert((2 * d - 4) * MAIN, 2 * MAIN)

    loop(1, 5, turn)

    await_rows(6)
    loop(1, 8, lambda i: over_copy(i).wait_recv())
    take_lo = mask(c128 == (r64 // 8) * 16 + r64 % 8)
    take_hi = mask(c128 == (r64 // 8) * 16 + 8 + r64 % 8)

    def unpack(n):
        got = ovrecv[:, tile(n)]
        xs[0, OVER : OVER + COL * NZ, tile(n)] = dot(take_lo, got).astype(BF)
        xs[1, OVER : OVER + COL * NZ, tile(n)] = dot(take_hi, got).astype(BF)

    loop(0, D // CW, unpack)
    expert(6 * MAIN, MAIN + COL * NZ)

    put_lo = mask((r128 % 16 < 8) & (c64 == (r128 // 16) * 8 + r128 % 16))
    put_hi = mask((r128 % 16 >= 8) & (c64 == (r128 // 16) * 8 + r128 % 16 - 8))
    over_rows = pl.ds(OVER, COL * NZ)

    def pack(n):
        lo, hi = retbuf[over_rows, tile(n)], retbuf[over_rows, tile(n + 4)]
        retov[:, tile(n)] = (dot(put_lo, lo) + dot(put_hi, hi)).astype(BF)

    loop(0, D // 2 // CW, pack)
    retov[:, D // 2 : OVB] = dot(put_lo, retbuf[over_rows, D:BACK]).astype(BF)
    loop(1, 8, lambda i: back_over_copy(i).start())
    retovr[rows16(s * 16, 16), :] = retov[rows16(s * 16, 16), :]

    def send_back(pos):
        loop(1, 8, lambda i: back_copy(pos, i).start())
        retrecv[pos, rows16(s * SLOT, SLOT), :] = retbuf[rows16(base(pos) + s * SLOT, SLOT), :]

    send_back(6)
    await_rows(7)
    expert(base(7), MAIN)
    send_back(7)

    def send_pair(k):
        send_back(4 - 2 * k)
        send_back(5 - 2 * k)

    loop(0, 2, send_pair)
    send_back(1)
    send_back(0)

    def weight_grad(j, m, emit):
        cols = pl.ds(pl.multiple_of(j * 512 + m * CW, CW), CW)
        emit(dot_tn(xs[0, :, cols], dgu[...]), dot_tn(xs[1, :, cols], hbuf[...]))

    def first_grads(m):
        def emit_to(slot):
            def emit(a, b):
                gsend[slot, tile(m), 0 : 2 * FF] = a.astype(BF)
                gsend[slot, tile(m), 2 * FF :] = b.astype(BF)

            return emit

        weight_grad((x + 2) % 4, m, emit_to(0))
        grad_copy(0, m, sgn).start()
        weight_grad((x - sgn + 4) % 4, m, emit_to(1))
        grad_copy(1, m, -sgn).start()

    loop(0, 2, first_grads)

    def own_grads(m):
        def emit(a, b):
            out_gu[tile(m), :] = a
            out_dn[tile(m), :] = b

        weight_grad(x, m, emit)

    loop(0, 2, own_grads)

    loop(1, 8, lambda i: back_over_copy(i).wait_recv())

    def unpack_back(n):
        got = retovr[:, tile(n)]
        rovf[0:64, tile(n)] = dot(take_lo, got).astype(BF)
        rovf[0:64, tile(n + 4)] = dot(take_hi, got).astype(BF)

    loop(0, D // 2 // CW, unpack_back)
    rovf[0:64, D:BACK] = dot(take_lo, retovr[:, D // 2 : OVB]).astype(BF)
    rovf[64:128, :] = jnp.zeros((64, BACK), BF)

    def combine(pos):
        loop(1, 8, lambda i: back_copy(pos, i).wait_recv())

        def column(n):
            tf[:, tile(n)] = dot(sel_t[pos], retrecv[pos, :, tile(n)]) + dot(sov_t[pos], rovf[:, tile(n)])

        loop(0, D // CW, column)
        tf[:, D:BACK] = dot(sel_t[pos], retrecv[pos, :, D:BACK]) + dot(sov_t[pos], rovf[:, D:BACK])

    def pass_on(pos, k, has_more):
        combine(pos)
        loop(1, 8, lambda i: back_copy(pos, i).wait_send())

        def piece(h):
            @pl.when(has_more)
            def _():
                sum_copy(pos + 2, h, k).wait_recv()

                def part(n):
                    at = rows16(h * 64 + n * 16, 16)
                    total = tf[at, :] + rsr[pos + 1, at, :].astype(F32)
                    retbuf[rows16(base(pos) + h * 64 + n * 16, 16), :] = total.astype(BF)

                loop(0, 4, part)

            @pl.when(jnp.logical_not(has_more))
            def _():
                def part(n):
                    at = rows16(h * 64 + n * 16, 16)
                    retbuf[rows16(base(pos) + h * 64 + n * 16, 16), :] = tf[at, :].astype(BF)

                loop(0, 4, part)

            sum_copy(pos, h, k).start()

        loop(0, 2, piece)

    def drain():
        far_copy().wait_send()
        loop(1, 8, lambda i: meta_copy(i).wait_send())
        loop(1, 8, lambda i: over_copy(i).wait_send())
        loop(1, 8, lambda i: back_over_copy(i).wait_send())

        def drain_rows(pos):
            loop(1, 8, lambda i: row_copy(pos, 0, i).wait_send())
            loop(1, 8, lambda i: row_copy(pos, 1, i).wait_send())

        loop(0, NZ, drain_rows)

        def drain_ring(pos):
            ag_copy(tok_ref, pos, 0, sgn).wait_send()
            ag_copy(tok_ref, pos, 1, sgn).wait_send()

        loop(1, 8, drain_ring)

    def back_turn(k):
        @pl.when(k < 3)
        def _():
            pass_on(6 - 2 * k, sgn, k > 0)

        pass_on(7 - 2 * k, -sgn, k > 0)

        @pl.when(k == 0)
        def _():
            drain()

        @pl.when((k == 1) | (k == 2))
        def _():
            m = k - 1
            grad_copy(0, m, sgn).wait()

            def emit(a, b):
                got = grecv[0, tile(m), :].astype(F32)
                gsend[0, tile(m), 0 : 2 * FF] = (a + got[:, 0 : 2 * FF]).astype(BF)
                gsend[0, tile(m), 2 * FF :] = (b + got[:, 2 * FF :]).astype(BF)

            weight_grad((x + sgn + 4) % 4, m, emit)
            grad_copy(2, m, sgn).start()

    loop(0, 4, back_turn)

    combine(0)
    for pos in (1, 2):
        for h in (0, 1):
            sum_copy(pos, h, sgn).wait_recv()

    def finish(n):
        at = rows16(n * 16, 16)
        total = tf[at, :] + rsr[0, at, :].astype(F32) + rsr[1, at, :].astype(F32)
        out_tok[at, :] = total[:, 0:D].astype(BF)
        tf[at, D:BACK] = total[:, D:BACK]

    loop(0, TOK // 16, finish)
    router = tf[:, D:BACK]
    by_lane = router.T
    rows = []
    for k in range(8):
        hit = ids_t[k : k + 1, :] == iota((128, TOK), 0)
        rows.append(jnp.sum(jnp.where(hit, by_lane, 0.0), axis=0, keepdims=True))
    out_prob[...] = (jnp.concatenate(rows, axis=0) / probs_t).astype(BF)

    for m in (0, 1):
        grad_copy(1, m, -sgn).wait()
        grad_copy(2, m, sgn).wait()

    def add_grads(n):
        at = rows16(n * 32, 32)
        more = grecv[1, at, :].astype(F32) + grecv[2, at, :].astype(F32)
        out_gu[at, :] = out_gu[at, :] + more[:, 0 : 2 * FF]
        out_dn[at, :] = out_dn[at, :] + more[:, 2 * FF :]

    loop(0, 512 // 32, add_grads)

    loop(1, 8, lambda i: back_copy(0, i).wait_send())

    def drain_sums(pos):
        sum_copy(pos, 0, sgn).wait_send()
        sum_copy(pos, 1, sgn).wait_send()

    loop(1, 8, drain_sums)


def copy_out(*refs):
    sources, targets, held, sems = refs[:4], refs[4:8], refs[8:12], refs[12]
    parts = [(0, 0, 128), (1, 0, 8)] + [(2, k * 128, 128) for k in range(4)] + [(3, k * 256, 256) for k in range(2)]

    def copy(at, which, a, b):
        n, start, count = parts[at]
        rows = pl.ds(start, count)
        return pltpu.make_async_copy(a[n].at[rows], b[n].at[rows], sems.at[which, at])

    for at in range(len(parts)):
        copy(at, 0, sources, held).start()
    for at in range(len(parts)):
        copy(at, 0, sources, held).wait()
        copy(at, 1, held, targets).start()
    for at in range(len(parts)):
        copy(at, 1, held, targets).wait()


def on_device(tokens, out_grad, expert_ids, route_probs, w_gate_up, w_down):
    vm, dma = pltpu.VMEM, pltpu.SemaphoreType.DMA
    inside = pl.BlockSpec(memory_space=pltpu.VMEM)
    token_grad, prob_grad, grad_gu, grad_dn = pl.pallas_call(
        kernel,
        out_shape=(
            jax.ShapeDtypeStruct((TOK, D), BF),
            jax.ShapeDtypeStruct((8, TOK), BF),
            jax.ShapeDtypeStruct((512, 2 * FF), F32),
            jax.ShapeDtypeStruct((512, FF), F32),
        ),
        in_specs=[inside] * 4 + [pl.BlockSpec(memory_space=pl.ANY)] * 2,
        out_specs=(inside,) * 4,
        scratch_shapes=[
            vm((D, 2 * FF), BF),
            vm((D, FF), BF),
            vm((NZ, 16, TOK), F32),
            vm((NZ, 16, TOK), F32),
            vm((16, D), BF),
            vm((16, D), BF),
            vm((2, NZ, MAIN + 16, TOK), BF),
            vm((NZ, TOK, MAIN), BF),
            vm((NZ, TOK, 128), BF),
            vm((NZ - 1, 2, TOK, D), BF),
            vm((NZ, 2, MAIN, D), BF),
            vm((2, 64, D), F32),
            vm((128, D), BF),
            vm((128, D), BF),
            vm((2, ROWS, D), BF),
            vm((320, 2 * FF), F32),
            vm((320, FF), F32),
            vm((ROWS, FF), BF),
            vm((ROWS, 2 * FF), BF),
            vm((ROWS, BACK), BF),
            vm((NZ, MAIN, BACK), BF),
            vm((128, OVB), BF),
            vm((128, OVB), BF),
            vm((128, BACK), BF),
            vm((TOK, BACK), F32),
            vm((NZ - 1, TOK, BACK), BF),
            vm((2, 512, 3 * FF), BF),
            vm((3, 512, 3 * FF), BF),
            dma((2,)),
            dma((2,)),
            dma((8,)), dma((8,)),
            dma((7, 2)), dma((7, 2)),
            dma((16, 8)), dma((16, 8)),
            dma((8,)), dma((8,)),
            dma((8, 8)), dma((8, 8)),
            dma((8,)), dma((8,)),
            dma((7, 2)), dma((7, 2)),
            dma((3, 2)), dma((3, 2)),
        ],
        compiler_params=pltpu.CompilerParams(
            collective_id=0, has_side_effects=True, vmem_limit_bytes=62 * 2**20
        ),
        cost_estimate=pl.CostEstimate(flops=15 * 10**9, bytes_accessed=10**7, transcendentals=10**6),
        name="routed_backward",
    )(tokens, out_grad, expert_ids.T, route_probs.T, w_gate_up[0], w_down[0])
    results = (token_grad, prob_grad, grad_gu, grad_dn)
    anywhere = pl.BlockSpec(memory_space=pltpu.HBM)
    token_grad, prob_grad, grad_gu, grad_dn = pl.pallas_call(
        copy_out,
        out_shape=tuple(jax.ShapeDtypeStruct(r.shape, r.dtype) for r in results),
        in_specs=[anywhere] * 4,
        out_specs=(anywhere,) * 4,
        scratch_shapes=[vm(r.shape, r.dtype) for r in results] + [dma((2, 8))],
        name="results",
    )(*results)
    return token_grad, prob_grad.T, grad_gu[None], grad_dn[None]


def solution(mesh):
    in_specs = (
        P(("expert", "dp"), None),
        P(("expert", "dp"), None),
        P(("expert", "dp"), None),
        P(("expert", "dp"), None),
        P("expert", None, None),
        P("expert", None, None),
    )
    out_specs = (
        P(("expert", "dp"), None),
        P(("expert", "dp"), None),
        P("expert", "dp", None),
        P("expert", "dp", None),
    )
    return jax.shard_map(
        on_device, mesh=mesh, in_specs=in_specs, out_specs=out_specs, check_vma=False
    )
```

```python
import functools

import jax
import jax.numpy as jnp
from jax import lax
from jax.experimental import pallas as pl
from jax.experimental.pallas import tpu as pltpu
from jax.sharding import PartitionSpec as P

MESH = pl.DeviceIdType.MESH
BF = jnp.bfloat16
F32 = jnp.float32

NZ = 8
COL = 8
TOK = 128
D = 2048
FF = 384
SLOT = 16
MAIN = COL * SLOT
ROWS = NZ * MAIN + COL * NZ
OVER = (NZ - 1) * MAIN
CW = 256


def iota(shape, dim):
    return lax.broadcasted_iota(jnp.int32, shape, dim)


def dot(a, b):
    return jnp.dot(a, b, preferred_element_type=F32)


def dot_nt(a, b):
    return lax.dot_general(a, b, (((1,), (1,)), ((), ())), preferred_element_type=F32)


def dot_tn(a, b):
    return lax.dot_general(a, b, (((0,), (0,)), ((), ())), preferred_element_type=F32)


def tile(n, width=CW):
    return pl.ds(pl.multiple_of(n * width, width), width)


def wide(n):
    return slice(n * 1024, n * 1024 + 1024)


def rows16(start, count):
    return pl.ds(pl.multiple_of(start, 16), count)


def mask(cond, dtype=BF):
    return jnp.where(cond, 1.0, 0.0).astype(dtype)


def kernel(
    tok_hbm, dy_hbm, ids_ref, probs_ref, wgu_hbm, wdn_hbm,
    out_tok, out_prob, out_gu, out_dn,
    tok_ref, dy_ref, wgu, wdn, meta_own, meta_all, far, far_in, sel, sel_t, sov_t, blk, sendbuf, ovf32, ovsend, ovrecv,
    xs, gu, hg, hbuf, dgu, retbuf, retrecv, retov, retovr, rovf, tf, rsr, gsend, grecv, qbuf, qin, gq, gall,
    w_sem, far_sem, meta_s, meta_r, ag_s, ag_r, d_s, d_r, ov_s, ov_r, r_s, r_r, ro_s, ro_r, rs_s, rs_r, g_s, g_r, q_s, q_r, p_s, p_r,
):
    e = lax.axis_index("expert")
    x = lax.axis_index("dp")
    y, z, c = e // 16, (e // 2) % 8, e % 2
    s = y * 2 + c
    sgn = 1 - 2 * c

    def zdev(k):
        return ((y * 8 + (z + k + 8) % 8) * 2 + c, x)

    def coldev(t):
        return (((t // 2) * 8 + z) * 2 + t % 2, x)

    other = [(s + i) % 8 for i in range(8)]
    other_dev = [coldev(t) for t in other]

    def xdev(k):
        return (e, (x + k + 4) % 4)

    def remote(src, dst, ss, rs, dev):
        return pltpu.make_async_remote_copy(
            src_ref=src, dst_ref=dst, send_sem=ss, recv_sem=rs, device_id=dev, device_id_type=MESH
        )

    def base(pos):
        return pos * MAIN + (pos // (NZ - 1)) * COL * NZ

    def loop(lo, hi, fn):
        def step(i, carry):
            fn(i)
            return carry

        lax.fori_loop(lo, hi, step, 0)

    def meta_copy(i):
        return remote(
            meta_own.at[(z + i) % 8], meta_all.at[i], meta_s.at[i], meta_r.at[i], zdev(i)
        )

    def ag_copy(src, pos, p, k):
        return remote(src, blk.at[pos - 1, p], ag_s.at[pos - 1, p], ag_r.at[pos - 1, p], zdev(k))

    def row_copy(pos, p, i):
        t, dev = (other[i], other_dev[i]) if isinstance(i, int) else (s, coldev((s + i) % 8))
        return remote(
            sendbuf.at[pos, p, rows16(t * SLOT, SLOT)],
            xs.at[p, rows16(base(pos) + s * SLOT, SLOT)],
            d_s.at[pos * 2 + p, i],
            d_r.at[pos * 2 + p, i],
            dev,
        )

    def over_copy(i):
        t = (s + i) % 8
        return remote(
            ovsend.at[rows16(t * 16, 16)], ovrecv.at[rows16(s * 16, 16)], ov_s.at[i], ov_r.at[i], coldev(t)
        )

    def back_copy(pos, i):
        t, dev = (other[i], other_dev[i]) if isinstance(i, int) else (s, coldev((s + i) % 8))
        return remote(
            retbuf.at[rows16(base(pos) + t * SLOT, SLOT)],
            retrecv.at[pos, rows16(s * SLOT, SLOT)],
            r_s.at[pos, i],
            r_r.at[pos, i],
            dev,
        )

    def back_over_copy(i):
        t = (s + i) % 8
        return remote(
            retov.at[rows16(t * 16, 16)], retovr.at[rows16(s * 16, 16)], ro_s.at[i], ro_r.at[i], coldev(t)
        )

    def sum_copy(pos, piece, k):
        return remote(
            retbuf.at[rows16(base(pos) + piece * 64, 64)],
            rsr.at[pos - 1, rows16(piece * 64, 64)],
            rs_s.at[pos - 1, piece],
            rs_r.at[pos - 1, piece],
            zdev(k),
        )

    def grad_copy(slot, half, k):
        return remote(
            gsend.at[slot % 2, tile(half)],
            grecv.at[slot, tile(half)],
            g_s.at[slot, half],
            g_r.at[slot, half],
            xdev(k),
        )

    def q_copy(i):
        t = (s + i) % 8
        return remote(qbuf.at[rows16(t * 16, 16)], qin.at[rows16(s * 16, 16)], q_s.at[i], q_r.at[i], coldev(t))

    def p_copy(pos):
        k = -sgn * ((pos + 1) // 2) if pos % 2 else sgn * (pos // 2)
        return remote(gq.at[pos], gall.at[z], p_s.at[pos], p_r.at[pos], zdev(k))

    def far_copy():
        return remote(far, far_in, far_sem.at[0], far_sem.at[1], zdev(4))

    barrier = pltpu.get_barrier_semaphore()
    for i in range(1, 8):
        pl.semaphore_signal(barrier, inc=1, device_id=zdev(i), device_id_type=MESH)
        pl.semaphore_signal(barrier, inc=1, device_id=coldev((s + i) % 8), device_id_type=MESH)
    for k in (-1, 1):
        pl.semaphore_signal(barrier, inc=1, device_id=xdev(k), device_id_type=MESH)
    x_copy = pltpu.make_async_copy(tok_hbm, tok_ref, w_sem.at[2])
    dy_copy = pltpu.make_async_copy(dy_hbm, dy_ref, w_sem.at[3])
    x_copy.start()
    dy_copy.start()
    w_gu_copy = pltpu.make_async_copy(wgu_hbm, wgu, w_sem.at[0])
    w_dn_copy = pltpu.make_async_copy(wdn_hbm, wdn, w_sem.at[1])
    w_gu_copy.start()
    w_dn_copy.start()
    qbuf[...] = jnp.zeros((192, 128), F32)

    def by_z(ids):
        return ((ids // 2) % 8) * 8 + (ids // 16) * 2 + ids % 2

    ids_t = by_z(ids_ref[...])
    probs_t = probs_ref[...].astype(F32)
    lane_of = iota((64, TOK), 0)
    named = jnp.zeros((64, TOK), F32)
    weight = jnp.zeros((64, TOK), F32)
    for k in range(8):
        hit = ids_t[k : k + 1, :] == lane_of
        named += jnp.where(hit, 1.0, 0.0)
        weight += jnp.where(hit, probs_t[k : k + 1, :], 0.0)
    before = mask(iota((TOK, TOK), 0) < iota((TOK, TOK), 1))
    rank = jnp.where(named > 0.0, dot(named.astype(BF), before), -1.0)
    for k in range(NZ):
        meta_own[k, 0:8, :] = rank[k * 8 : k * 8 + 8]
        meta_own[k, 8:16, :] = weight[k * 8 : k * 8 + 8]

    def build(pos, info):
        ranks, weights = info[0:8], info[8:16]

        def spread(a, n):
            return jnp.concatenate([jnp.broadcast_to(a[k : k + 1], (n, TOK)) for k in range(8)], axis=0)

        hit = spread(ranks, SLOT) == (iota((MAIN, TOK), 0) % SLOT).astype(F32)
        over = ranks == float(SLOT)
        none = jnp.zeros((8, TOK), F32)
        one = jnp.where(hit, 1.0, 0.0)
        sel[0, pos, 0:MAIN, :] = one.astype(BF)
        sel[0, pos, MAIN : MAIN + 16, :] = jnp.concatenate([jnp.where(over, 1.0, 0.0), none], axis=0).astype(BF)
        sel[1, pos, 0:MAIN, :] = jnp.where(hit, spread(weights, SLOT), 0.0).astype(BF)
        sel[1, pos, MAIN : MAIN + 16, :] = jnp.concatenate([jnp.where(over, weights, 0.0), none], axis=0).astype(BF)
        sel_t[pos] = one.T.astype(BF)
        mine = (spread(ranks, 8) == float(SLOT)) & (iota((64, TOK), 0) % 8 == pos)
        wide = jnp.concatenate([jnp.where(mine, 1.0, 0.0), jnp.zeros((64, TOK), F32)], axis=0)
        sov_t[pos] = wide.T.astype(BF)

    def pick(pos, p, ref):
        for n in (0, 1):
            got = dot(sel[p, pos], ref[:, wide(n)])
            sendbuf[pos, p, :, wide(n)] = got[:MAIN].astype(BF)
            ovf32[p, pl.ds(pl.multiple_of(pos * 8, 8), 8), wide(n)] = got[MAIN : MAIN + 8]

    def send(pos, p):
        for i in range(1, 8):
            row_copy(pos, p, i).start()
        xs[p, rows16(base(pos) + s * SLOT, SLOT), :] = sendbuf[pos, p, rows16(s * SLOT, SLOT), :]

    def await_half(pos, p):
        for i in range(1, 8):
            row_copy(pos, p, i).wait_recv()

    def await_rows(pos):
        await_half(pos, 0)
        await_half(pos, 1)

    def expert(row0, count, places, between=lambda: None):
        rows = rows16(row0, count)
        gu[0:count, :] = dot(xs[0, rows, :], wgu[...])
        between()
        hg[0:count, :] = dot(xs[1, rows, :], wdn[...])

        def middle(n, place, lane):
            part, whole = rows16(n * 64, 64), rows16(row0 + n * 64, 64)
            gate, up, grad = gu[part, 0:FF], gu[part, FF : 2 * FF], hg[part, :]
            sig = jax.nn.sigmoid(gate)
            silu = gate * sig
            act = (silu * up).astype(BF)
            hbuf[whole, :] = act
            dgu[whole, 0:FF] = (grad * up * sig * (1.0 + gate * (1.0 - sig))).astype(BF)
            dgu[whole, FF : 2 * FF] = (grad * silu).astype(BF)
            router = jnp.sum(grad * act.astype(F32), axis=1, keepdims=True)
            at = pl.ds(pl.multiple_of(place, 16), 64)
            qbuf[at, :] = qbuf[at, :] + jnp.where(iota((64, 128), 1) == lane, router, 0.0)

        for lo, hi, place in places:
            loop(lo, hi, lambda n, place=place: middle(n, *place(n)))

        def last(n):
            retbuf[rows, tile(n, 512)] = dot_nt(dgu[rows, :], wgu[tile(n, 512), :]).astype(BF)

        loop(0, D // 512, last)

    build(0, meta_own[z])
    x_copy.wait()
    pick(0, 0, tok_ref)

    pl.semaphore_wait(barrier, 16)

    ag_copy(tok_ref, 1, 0, sgn).start()
    ag_copy(tok_ref, 2, 0, -sgn).start()
    send(0, 0)
    loop(1, 8, lambda i: meta_copy(i).start())
    dy_copy.wait()
    ag_copy(dy_ref, 1, 1, sgn).start()
    ag_copy(dy_ref, 2, 1, -sgn).start()
    pick(0, 1, dy_ref)
    send(0, 1)

    opposite = meta_own[(z + 4) % 8]
    nobody = jnp.zeros((8, TOK), F32)
    far_one = jnp.concatenate([jnp.where(opposite[0:8] == float(SLOT), 1.0, 0.0), nobody], axis=0).astype(BF)
    far_weight = jnp.concatenate([nobody, jnp.where(opposite[0:8] == float(SLOT), opposite[8:16], 0.0)], axis=0).astype(BF)

    for n in (0, 1):
        far[:, wide(n)] = (dot(far_one, tok_ref[:, wide(n)]) + dot(far_weight, dy_ref[:, wide(n)])).astype(BF)
    far_copy().start()
    w_gu_copy.wait()
    w_dn_copy.wait()

    r128, c64 = iota((128, 64), 0), iota((128, 64), 1)
    r64, c128 = iota((64, 128), 0), iota((64, 128), 1)

    def pair(pos):
        await_rows(pos)
        await_rows(pos + 1)
        expert(pos * MAIN, 2 * MAIN, [(0, 4, lambda n: ((n % 2) * 64, (pos + n // 2) * 8 + s))])

    def turn(d):
        odd, even = 2 * d - 1, 2 * d
        up_at, down_at = (8 + sgn * d) % 8, (8 - sgn * d) % 8
        meta_copy(up_at).wait_recv()
        build(odd, meta_all[up_at])

        @pl.when(d < 4)
        def _():
            meta_copy(down_at).wait_recv()
            build(even, meta_all[down_at])

        def piece(p):
            @pl.when((p == 1) & (d >= 2) & (d < 4))
            def _():
                pair(2 * d - 4)

            ag_copy(tok_ref, odd, p, sgn).wait_recv()

            @pl.when(d < 4)
            def _():
                ag_copy(blk.at[odd - 1, p], odd + 2, p, sgn).start()

            pick(odd, p, blk.at[odd - 1, p])
            send(odd, p)

            @pl.when(d < 4)
            def _():
                ag_copy(tok_ref, even, p, -sgn).wait_recv()

                @pl.when(d < 3)
                def _():
                    ag_copy(blk.at[even - 1, p], even + 2, p, -sgn).start()

                pick(even, p, blk.at[even - 1, p])
                send(even, p)

        loop(0, 2, piece)

        @pl.when(d == 3)
        def _():
            far_copy().wait_recv()
            ovf32[0, 56:64, :] = far_in[...].astype(F32)[0:8]
            ovf32[1, 56:64, :] = far_in[...].astype(F32)[8:16]
            where_of = c64 == (r128 % 8) * 8 + r128 // 16
            first, second = mask((r128 % 16 < 8) & where_of), mask((r128 % 16 >= 8) & where_of)

            for n in (0, 1):
                a, b = ovf32[0, :, wide(n)].astype(BF), ovf32[1, :, wide(n)].astype(BF)
                ovsend[:, wide(n)] = (dot(first, a) + dot(second, b)).astype(BF)
            loop(1, 8, lambda i: over_copy(i).start())
            ovrecv[rows16(s * 16, 16), :] = ovsend[rows16(s * 16, 16), :]


    loop(1, 5, turn)

    pair(4)
    await_rows(6)
    loop(1, 8, lambda i: over_copy(i).wait_recv())
    take_lo = mask(c128 == (r64 // 8) * 16 + r64 % 8)
    take_hi = mask(c128 == (r64 // 8) * 16 + 8 + r64 % 8)

    for n in (0, 1):
        got = ovrecv[:, wide(n)]
        xs[0, OVER : OVER + COL * NZ, wide(n)] = dot(take_lo, got).astype(BF)
        xs[1, OVER : OVER + COL * NZ, wide(n)] = dot(take_hi, got).astype(BF)
    expert(
        6 * MAIN,
        MAIN + COL * NZ,
        [(0, 2, lambda n: (n * 64, 48 + s)), (2, 3, lambda n: (n * 64, 64 + s))],
    )

    put_lo = mask((r128 % 16 < 8) & (c64 == (r128 // 16) * 8 + r128 % 16))
    put_hi = mask((r128 % 16 >= 8) & (c64 == (r128 // 16) * 8 + r128 % 16 - 8))
    over_rows = pl.ds(OVER, COL * NZ)

    retov[...] = (dot(put_lo, retbuf[over_rows, wide(0)]) + dot(put_hi, retbuf[over_rows, wide(1)])).astype(BF)
    loop(1, 8, lambda i: back_over_copy(i).start())
    retovr[rows16(s * 16, 16), :] = retov[rows16(s * 16, 16), :]

    def send_back(pos):
        for i in range(1, 8):
            back_copy(pos, i).start()
        retrecv[pos, rows16(s * SLOT, SLOT), :] = retbuf[rows16(base(pos) + s * SLOT, SLOT), :]

    send_back(6)
    await_half(7, 0)
    expert(base(7), MAIN, [(0, 2, lambda n: (n * 64, 56 + s))], lambda: await_half(7, 1))
    send_back(7)
    for t in range(8):
        qbuf[t * 16 : t * 16 + 8, :] = qbuf[t * 16 : t * 16 + 8, :] + qbuf[MAIN + t * 8 : MAIN + t * 8 + 8, :]
    loop(1, 8, lambda i: q_copy(i).start())
    qin[rows16(s * 16, 16), :] = qbuf[rows16(s * 16, 16), :]

    def send_pair(k):
        send_back(4 - 2 * k)
        send_back(5 - 2 * k)

    loop(0, 2, send_pair)
    send_back(1)
    send_back(0)

    def weight_grad(j, m, emit):
        cols = pl.ds(pl.multiple_of(j * 512 + m * CW, CW), CW)
        emit(dot_tn(xs[0, :, cols], dgu[...]), dot_tn(xs[1, :, cols], hbuf[...]))

    def first_grads(m):
        def emit_to(slot):
            def emit(a, b):
                gsend[slot, tile(m), 0 : 2 * FF] = a.astype(BF)
                gsend[slot, tile(m), 2 * FF :] = b.astype(BF)

            return emit

        weight_grad((x + 2) % 4, m, emit_to(0))
        grad_copy(0, m, sgn).start()
        weight_grad((x - sgn + 4) % 4, m, emit_to(1))
        grad_copy(1, m, -sgn).start()

    loop(0, 2, first_grads)

    def own_grads(m):
        def emit(a, b):
            out_gu[tile(m), :] = a
            out_dn[tile(m), :] = b

        weight_grad(x, m, emit)

    loop(0, 2, own_grads)

    loop(1, 8, lambda i: back_over_copy(i).wait_recv())

    got_back = retovr[...]
    rovf[0:64, wide(0)] = dot(take_lo, got_back).astype(BF)
    rovf[0:64, wide(1)] = dot(take_hi, got_back).astype(BF)
    rovf[64:128, :] = jnp.zeros((64, D), BF)

    def combine(pos):
        for i in range(1, 8):
            back_copy(pos, i).wait_recv()

        for n in (0, 1):
            tf[:, wide(n)] = dot(sel_t[pos], retrecv[pos, :, wide(n)]) + dot(sov_t[pos], rovf[:, wide(n)])

    def pass_on(pos, k, has_more):
        combine(pos)
        for i in range(1, 8):
            back_copy(pos, i).wait_send()

        def piece(h):
            @pl.when(has_more)
            def _():
                sum_copy(pos + 2, h, k).wait_recv()

                def part(n):
                    at = rows16(h * 64 + n * 16, 16)
                    total = tf[at, :] + rsr[pos + 1, at, :].astype(F32)
                    retbuf[rows16(base(pos) + h * 64 + n * 16, 16), :] = total.astype(BF)

                loop(0, 4, part)

            @pl.when(jnp.logical_not(has_more))
            def _():
                def part(n):
                    at = rows16(h * 64 + n * 16, 16)
                    retbuf[rows16(base(pos) + h * 64 + n * 16, 16), :] = tf[at, :].astype(BF)

                loop(0, 4, part)

            sum_copy(pos, h, k).start()

        loop(0, 2, piece)

    def add_grads(slot):
        def part(n):
            at = rows16(n * 32, 32)
            more = grecv[slot, at, :].astype(F32)
            out_gu[at, :] = out_gu[at, :] + more[:, 0 : 2 * FF]
            out_dn[at, :] = out_dn[at, :] + more[:, 2 * FF :]

        loop(0, 512 // 32, part)

    def drain():
        far_copy().wait_send()
        loop(1, 8, lambda i: meta_copy(i).wait_send())
        loop(1, 8, lambda i: over_copy(i).wait_send())
        loop(1, 8, lambda i: back_over_copy(i).wait_send())

        def drain_rows(pos):
            loop(1, 8, lambda i: row_copy(pos, 0, i).wait_send())
            loop(1, 8, lambda i: row_copy(pos, 1, i).wait_send())

        loop(0, NZ, drain_rows)

        def drain_ring(pos):
            ag_copy(tok_ref, pos, 0, sgn).wait_send()
            ag_copy(tok_ref, pos, 1, sgn).wait_send()

        loop(1, 8, drain_ring)

    def routers():
        loop(1, 8, lambda i: q_copy(i).wait_recv())
        held = qin[0:16, :]
        for o in range(1, 8):
            held = held + qin[o * 16 : o * 16 + 16, :]
        for pos in range(NZ):
            one = sel[0, pos, :, :].astype(F32)
            rows = []
            for o in range(8):
                value = held[:, pos * 8 + o : pos * 8 + o + 1]
                row = jnp.sum(one[o * 16 : o * 16 + 16] * value, axis=0, keepdims=True)
                rows.append(row + one[MAIN + o : MAIN + o + 1] * held[pos : pos + 1, 64 + o : 65 + o])
            gq[pos] = jnp.concatenate(rows, axis=0)
        for pos in range(1, NZ):
            p_copy(pos).start()
        gall[z] = gq[0]

    def back_turn(k):
        @pl.when(k < 3)
        def _():
            pass_on(6 - 2 * k, sgn, k > 0)

        pass_on(7 - 2 * k, -sgn, k > 0)

        @pl.when(k < 2)
        def _():
            m = k
            grad_copy(0, m, sgn).wait()

            def emit(a, b):
                got = grecv[0, tile(m), :].astype(F32)
                gsend[0, tile(m), 0 : 2 * FF] = (a + got[:, 0 : 2 * FF]).astype(BF)
                gsend[0, tile(m), 2 * FF :] = (b + got[:, 2 * FF :]).astype(BF)

            weight_grad((x + sgn + 4) % 4, m, emit)
            grad_copy(2, m, sgn).start()

        @pl.when(k == 0)
        def _():
            routers()

        @pl.when(k == 1)
        def _():
            drain()

        @pl.when(k == 2)
        def _():
            for m in (0, 1):
                grad_copy(1, m, -sgn).wait()
            add_grads(1)

    loop(0, 4, back_turn)

    combine(0)
    for pos in (1, 2):
        for h in (0, 1):
            sum_copy(pos, h, sgn).wait_recv()

    def finish(n):
        at = rows16(n * 16, 16)
        total = tf[at, :] + rsr[0, at, :].astype(F32) + rsr[1, at, :].astype(F32)
        out_tok[at, :] = total.astype(BF)

    loop(0, TOK // 16, finish)
    for pos in range(1, NZ):
        p_copy(pos).wait()
    by_lane = gall[...].reshape(64, TOK)
    rows = []
    for k in range(8):
        hit = ids_t[k : k + 1, :] == lane_of
        rows.append(jnp.sum(jnp.where(hit, by_lane, 0.0), axis=0, keepdims=True))
    out_prob[...] = (jnp.concatenate(rows, axis=0) / probs_t).astype(BF)

    for m in (0, 1):
        grad_copy(2, m, sgn).wait()
    add_grads(2)

    loop(1, 8, lambda i: back_copy(0, i).wait_send())
    loop(1, 8, lambda i: q_copy(i).wait_send())

    def drain_sums(pos):
        sum_copy(pos, 0, sgn).wait_send()
        sum_copy(pos, 1, sgn).wait_send()

    loop(1, 8, drain_sums)


def copy_out(*refs):
    sources, targets, held, sems = refs[:4], refs[4:8], refs[8:12], refs[12]
    parts = [(0, 0, 128), (1, 0, 8)] + [(2, k * 128, 128) for k in range(4)] + [(3, k * 256, 256) for k in range(2)]

    def copy(at, which, a, b):
        n, start, count = parts[at]
        rows = pl.ds(start, count)
        return pltpu.make_async_copy(a[n].at[rows], b[n].at[rows], sems.at[which, at])

    for at in range(len(parts)):
        copy(at, 0, sources, held).start()
    for at in range(len(parts)):
        copy(at, 0, sources, held).wait()
        copy(at, 1, held, targets).start()
    for at in range(len(parts)):
        copy(at, 1, held, targets).wait()


def on_device(tokens, out_grad, expert_ids, route_probs, w_gate_up, w_down):
    vm, dma = pltpu.VMEM, pltpu.SemaphoreType.DMA
    inside = pl.BlockSpec(memory_space=pltpu.VMEM)
    token_grad, prob_grad, grad_gu, grad_dn = pl.pallas_call(
        kernel,
        out_shape=(
            jax.ShapeDtypeStruct((TOK, D), BF),
            jax.ShapeDtypeStruct((8, TOK), BF),
            jax.ShapeDtypeStruct((512, 2 * FF), F32),
            jax.ShapeDtypeStruct((512, FF), F32),
        ),
        in_specs=[pl.BlockSpec(memory_space=pl.ANY)] * 2 + [inside] * 2 + [pl.BlockSpec(memory_space=pl.ANY)] * 2,
        out_specs=(inside,) * 4,
        scratch_shapes=[
            vm((TOK, D), BF),
            vm((TOK, D), BF),
            vm((D, 2 * FF), BF),
            vm((D, FF), BF),
            vm((NZ, 16, TOK), F32),
            vm((NZ, 16, TOK), F32),
            vm((16, D), BF),
            vm((16, D), BF),
            vm((2, NZ, MAIN + 16, TOK), BF),
            vm((NZ, TOK, MAIN), BF),
            vm((NZ, TOK, 128), BF),
            vm((NZ - 1, 2, TOK, D), BF),
            vm((NZ, 2, MAIN, D), BF),
            vm((2, 64, D), F32),
            vm((128, D), BF),
            vm((128, D), BF),
            vm((2, ROWS, D), BF),
            vm((320, 2 * FF), F32),
            vm((320, FF), F32),
            vm((ROWS, FF), BF),
            vm((ROWS, 2 * FF), BF),
            vm((ROWS, D), BF),
            vm((NZ, MAIN, D), BF),
            vm((128, D // 2), BF),
            vm((128, D // 2), BF),
            vm((128, D), BF),
            vm((TOK, D), F32),
            vm((NZ - 1, TOK, D), BF),
            vm((2, 512, 3 * FF), BF),
            vm((3, 512, 3 * FF), BF),
            vm((192, 128), F32),
            vm((128, 128), F32),
            vm((NZ, 8, TOK), F32),
            vm((NZ, 8, TOK), F32),
            dma((4,)),
            dma((2,)),
            dma((8,)), dma((8,)),
            dma((7, 2)), dma((7, 2)),
            dma((16, 8)), dma((16, 8)),
            dma((8,)), dma((8,)),
            dma((8, 8)), dma((8, 8)),
            dma((8,)), dma((8,)),
            dma((7, 2)), dma((7, 2)),
            dma((3, 2)), dma((3, 2)),
            dma((8,)), dma((8,)),
            dma((8,)), dma((8,)),
        ],
        compiler_params=pltpu.CompilerParams(
            collective_id=0, has_side_effects=True, vmem_limit_bytes=62 * 2**20
        ),
        cost_estimate=pl.CostEstimate(flops=15 * 10**9, bytes_accessed=10**7, transcendentals=10**6),
        name="routed_backward",
    )(tokens, out_grad, expert_ids.T, route_probs.T, w_gate_up[0], w_down[0])
    results = (token_grad, prob_grad, grad_gu, grad_dn)
    anywhere = pl.BlockSpec(memory_space=pltpu.HBM)
    token_grad, prob_grad, grad_gu, grad_dn = pl.pallas_call(
        copy_out,
        out_shape=tuple(jax.ShapeDtypeStruct(r.shape, r.dtype) for r in results),
        in_specs=[anywhere] * 4,
        out_specs=(anywhere,) * 4,
        scratch_shapes=[vm(r.shape, r.dtype) for r in results] + [dma((2, 8))],
        name="results",
    )(*results)
    return token_grad, prob_grad.T, grad_gu[None], grad_dn[None]


def solution(mesh):
    in_specs = (
        P(("expert", "dp"), None),
        P(("expert", "dp"), None),
        P(("expert", "dp"), None),
        P(("expert", "dp"), None),
        P("expert", None, None),
        P("expert", None, None),
    )
    out_specs = (
        P(("expert", "dp"), None),
        P(("expert", "dp"), None),
        P("expert", "dp", None),
        P("expert", "dp", None),
    )
    return jax.shard_map(
        on_device, mesh=mesh, in_specs=in_specs, out_specs=out_specs, check_vma=False
    )
```

```python
import functools

import jax
import jax.numpy as jnp
from jax import lax
from jax.experimental import pallas as pl
from jax.experimental.pallas import tpu as pltpu
from jax.sharding import PartitionSpec as P

MESH = pl.DeviceIdType.MESH
BF = jnp.bfloat16
F32 = jnp.float32

NZ = 8
COL = 8
TOK = 128
D = 2048
FF = 384
SLOT = 16
MAIN = COL * SLOT
ROWS = NZ * MAIN + COL * NZ
OVER = (NZ - 1) * MAIN
CW = 256


def iota(shape, dim):
    return lax.broadcasted_iota(jnp.int32, shape, dim)


def dot(a, b):
    return jnp.dot(a, b, preferred_element_type=F32)


def dot_nt(a, b):
    return lax.dot_general(a, b, (((1,), (1,)), ((), ())), preferred_element_type=F32)


def dot_tn(a, b):
    return lax.dot_general(a, b, (((0,), (0,)), ((), ())), preferred_element_type=F32)


def tile(n, width=CW):
    return pl.ds(pl.multiple_of(n * width, width), width)


def wide(n):
    return slice(n * 1024, n * 1024 + 1024)


def rows16(start, count):
    return pl.ds(pl.multiple_of(start, 16), count)


def mask(cond, dtype=BF):
    return jnp.where(cond, 1.0, 0.0).astype(dtype)


def kernel(
    tok_hbm, dy_hbm, ids_ref, probs_ref, wgu_hbm, wdn_hbm,
    out_tok, out_prob, gu_hbm, dn_hbm,
    out_gu, out_dn, own, wgu, wdn, meta_own, meta_all, far, far_in, sel, sel_t, sov_t, blk, sendbuf, ovf32, ovsend, ovrecv,
    xs, gu, hg, hbuf, dgu, retbuf, retrecv, retov, retovr, rovf, tf, rsr, gsend, grecv, qbuf, qin, gq, gall,
    w_sem, far_sem, meta_s, meta_r, ag_s, ag_r, d_s, d_r, ov_s, ov_r, r_s, r_r, ro_s, ro_r, rs_s, rs_r, g_s, g_r, q_s, q_r, p_s, p_r,
):
    e = lax.axis_index("expert")
    x = lax.axis_index("dp")
    y, z, c = e // 16, (e // 2) % 8, e % 2
    s = y * 2 + c
    sgn = 1 - 2 * c

    def zdev(k):
        return ((y * 8 + (z + k + 8) % 8) * 2 + c, x)

    def coldev(t):
        return (((t // 2) * 8 + z) * 2 + t % 2, x)

    other = [(s + i) % 8 for i in range(8)]
    other_dev = [coldev(t) for t in other]

    def xdev(k):
        return (e, (x + k + 4) % 4)

    def remote(src, dst, ss, rs, dev):
        return pltpu.make_async_remote_copy(
            src_ref=src, dst_ref=dst, send_sem=ss, recv_sem=rs, device_id=dev, device_id_type=MESH
        )

    def base(pos):
        return pos * MAIN + (pos // (NZ - 1)) * COL * NZ

    def loop(lo, hi, fn):
        def step(i, carry):
            fn(i)
            return carry

        lax.fori_loop(lo, hi, step, 0)

    def meta_copy(i):
        return remote(
            meta_own.at[(z + i) % 8], meta_all.at[i], meta_s.at[i], meta_r.at[i], zdev(i)
        )

    def ag_copy(src, pos, p, k):
        return remote(src, blk.at[pos - 1, p], ag_s.at[pos - 1, p], ag_r.at[pos - 1, p], zdev(k))

    def row_copy(pos, p, i):
        t, dev = (other[i], other_dev[i]) if isinstance(i, int) else (s, coldev((s + i) % 8))
        return remote(
            sendbuf.at[pos, p, rows16(t * SLOT, SLOT)],
            xs.at[p // 2, rows16(base(pos) + s * SLOT, SLOT), tile(p % 2, 1024)],
            d_s.at[pos * 4 + p, i],
            d_r.at[pos * 4 + p, i],
            dev,
        )

    def over_copy(i):
        t = (s + i) % 8
        return remote(
            ovsend.at[rows16(t * 16, 16)], ovrecv.at[rows16(s * 16, 16)], ov_s.at[i], ov_r.at[i], coldev(t)
        )

    def back_copy(pos, i):
        t, dev = (other[i], other_dev[i]) if isinstance(i, int) else (s, coldev((s + i) % 8))
        return remote(
            retbuf.at[rows16(base(pos) + t * SLOT, SLOT)],
            retrecv.at[pos, rows16(s * SLOT, SLOT)],
            r_s.at[pos, i],
            r_r.at[pos, i],
            dev,
        )

    def back_over_copy(i):
        t = (s + i) % 8
        return remote(
            retov.at[rows16(t * 16, 16)], retovr.at[rows16(s * 16, 16)], ro_s.at[i], ro_r.at[i], coldev(t)
        )

    def sum_copy(pos, piece, k):
        return remote(
            retbuf.at[rows16(base(pos) + piece * 64, 64)],
            rsr.at[pos - 1, rows16(piece * 64, 64)],
            rs_s.at[pos - 1, piece],
            rs_r.at[pos - 1, piece],
            zdev(k),
        )

    def grad_copy(slot, half, k):
        return remote(
            gsend.at[slot % 2, tile(half)],
            grecv.at[slot, tile(half)],
            g_s.at[slot, half],
            g_r.at[slot, half],
            xdev(k),
        )

    def q_copy(i):
        t = (s + i) % 8
        return remote(qbuf.at[rows16(t * 16, 16)], qin.at[rows16(s * 16, 16)], q_s.at[i], q_r.at[i], coldev(t))

    def p_copy(pos):
        k = -sgn * ((pos + 1) // 2) if pos % 2 else sgn * (pos // 2)
        return remote(gq.at[pos], gall.at[z], p_s.at[pos], p_r.at[pos], zdev(k))

    def far_copy():
        return remote(far, far_in, far_sem.at[0], far_sem.at[1], zdev(4))

    barrier = pltpu.get_barrier_semaphore()
    for i in range(1, 8):
        pl.semaphore_signal(barrier, inc=1, device_id=zdev(i), device_id_type=MESH)
        pl.semaphore_signal(barrier, inc=1, device_id=coldev((s + i) % 8), device_id_type=MESH)
    for k in (-1, 1):
        pl.semaphore_signal(barrier, inc=1, device_id=xdev(k), device_id_type=MESH)
    own_copies = [
        pltpu.make_async_copy((tok_hbm, tok_hbm, dy_hbm, dy_hbm)[p].at[:, wide(p % 2)], own.at[p], w_sem.at[2 + p])
        for p in range(4)
    ]
    for one_copy in own_copies:
        one_copy.start()
    w_gu_copy = pltpu.make_async_copy(wgu_hbm, wgu, w_sem.at[0])
    w_dn_copy = pltpu.make_async_copy(wdn_hbm, wdn, w_sem.at[1])
    w_gu_copy.start()
    w_dn_copy.start()
    qbuf[...] = jnp.zeros((192, 128), F32)

    def by_z(ids):
        return ((ids // 2) % 8) * 8 + (ids // 16) * 2 + ids % 2

    ids_t = by_z(ids_ref[...])
    probs_t = probs_ref[...].astype(F32)
    lane_of = iota((64, TOK), 0)
    named = jnp.zeros((64, TOK), F32)
    weight = jnp.zeros((64, TOK), F32)
    for k in range(8):
        hit = ids_t[k : k + 1, :] == lane_of
        named += jnp.where(hit, 1.0, 0.0)
        weight += jnp.where(hit, probs_t[k : k + 1, :], 0.0)
    before = mask(iota((TOK, TOK), 0) < iota((TOK, TOK), 1))
    rank = jnp.where(named > 0.0, dot(named.astype(BF), before), -1.0)
    for k in range(NZ):
        meta_own[k, 0:8, :] = rank[k * 8 : k * 8 + 8]
        meta_own[k, 8:16, :] = weight[k * 8 : k * 8 + 8]

    def build(pos, info):
        ranks, weights = info[0:8], info[8:16]

        def spread(a, n):
            return jnp.concatenate([jnp.broadcast_to(a[k : k + 1], (n, TOK)) for k in range(8)], axis=0)

        hit = spread(ranks, SLOT) == (iota((MAIN, TOK), 0) % SLOT).astype(F32)
        over = ranks == float(SLOT)
        none = jnp.zeros((8, TOK), F32)
        one = jnp.where(hit, 1.0, 0.0)
        sel[0, pos, 0:MAIN, :] = one.astype(BF)
        sel[0, pos, MAIN : MAIN + 16, :] = jnp.concatenate([jnp.where(over, 1.0, 0.0), none], axis=0).astype(BF)
        sel[1, pos, 0:MAIN, :] = jnp.where(hit, spread(weights, SLOT), 0.0).astype(BF)
        sel[1, pos, MAIN : MAIN + 16, :] = jnp.concatenate([jnp.where(over, weights, 0.0), none], axis=0).astype(BF)
        sel_t[pos] = one.T.astype(BF)
        mine = (spread(ranks, 8) == float(SLOT)) & (iota((64, TOK), 0) % 8 == pos)
        wide = jnp.concatenate([jnp.where(mine, 1.0, 0.0), jnp.zeros((64, TOK), F32)], axis=0)
        sov_t[pos] = wide.T.astype(BF)

    def pick(pos, p, ref):
        got = dot(sel[p // 2, pos], ref[...])
        sendbuf[pos, p] = got[:MAIN].astype(BF)
        ovf32[p // 2, pl.ds(pl.multiple_of(pos * 8, 8), 8), tile(p % 2, 1024)] = got[MAIN : MAIN + 8]

    def send(pos, p):
        for i in range(1, 8):
            row_copy(pos, p, i).start()
        xs[p // 2, rows16(base(pos) + s * SLOT, SLOT), tile(p % 2, 1024)] = sendbuf[pos, p, rows16(s * SLOT, SLOT), :]

    def await_half(pos, p):
        for i in range(1, 8):
            row_copy(pos, 2 * p, i).wait_recv()
            row_copy(pos, 2 * p + 1, i).wait_recv()

    def await_rows(pos):
        await_half(pos, 0)
        await_half(pos, 1)

    def expert(row0, count, places, between=lambda: None):
        rows = rows16(row0, count)
        gu[0:count, :] = dot(xs[0, rows, :], wgu[...])
        between()
        hg[0:count, :] = dot(xs[1, rows, :], wdn[...])

        def middle(n, place, lane):
            part, whole = rows16(n * 64, 64), rows16(row0 + n * 64, 64)
            gate, up, grad = gu[part, 0:FF], gu[part, FF : 2 * FF], hg[part, :]
            sig = jax.nn.sigmoid(gate)
            silu = gate * sig
            act = (silu * up).astype(BF)
            hbuf[whole, :] = act
            dgu[whole, 0:FF] = (grad * up * sig * (1.0 + gate * (1.0 - sig))).astype(BF)
            dgu[whole, FF : 2 * FF] = (grad * silu).astype(BF)
            router = jnp.sum(grad * act.astype(F32), axis=1, keepdims=True)
            at = pl.ds(pl.multiple_of(place, 16), 64)
            qbuf[at, :] = qbuf[at, :] + jnp.where(iota((64, 128), 1) == lane, router, 0.0)

        for lo, hi, place in places:
            loop(lo, hi, lambda n, place=place: middle(n, *place(n)))

        def last(n):
            retbuf[rows, tile(n, 512)] = dot_nt(dgu[rows, :], wgu[tile(n, 512), :]).astype(BF)

        loop(0, D // 512, last)

    build(0, meta_own[z])
    own_copies[0].wait()
    pick(0, 0, own.at[0])

    pl.semaphore_wait(barrier, 16)

    def own_ring(p):
        ag_copy(own.at[p], 1, p, sgn).start()
        ag_copy(own.at[p], 2, p, -sgn).start()

    loop(1, 8, lambda i: meta_copy(i).start())
    own_ring(0)
    send(0, 0)
    for p in (1, 2, 3):
        own_copies[p].wait()
        own_ring(p)
    for p in (1, 2, 3):
        pick(0, p, own.at[p])
        send(0, p)

    opposite = meta_own[(z + 4) % 8]
    nobody = jnp.zeros((8, TOK), F32)
    far_one = jnp.concatenate([jnp.where(opposite[0:8] == float(SLOT), 1.0, 0.0), nobody], axis=0).astype(BF)
    far_weight = jnp.concatenate([nobody, jnp.where(opposite[0:8] == float(SLOT), opposite[8:16], 0.0)], axis=0).astype(BF)

    for n in (0, 1):
        far[:, wide(n)] = (dot(far_one, own[n]) + dot(far_weight, own[2 + n])).astype(BF)
    far_copy().start()
    w_gu_copy.wait()
    w_dn_copy.wait()

    r128, c64 = iota((128, 64), 0), iota((128, 64), 1)
    r64, c128 = iota((64, 128), 0), iota((64, 128), 1)

    def pair(pos):
        await_rows(pos)
        await_rows(pos + 1)
        expert(pos * MAIN, 2 * MAIN, [(0, 4, lambda n: ((n % 2) * 64, (pos + n // 2) * 8 + s))])

    def turn(d):
        odd, even = 2 * d - 1, 2 * d
        up_at, down_at = (8 + sgn * d) % 8, (8 - sgn * d) % 8
        meta_copy(up_at).wait_recv()
        build(odd, meta_all[up_at])

        @pl.when(d < 4)
        def _():
            meta_copy(down_at).wait_recv()
            build(even, meta_all[down_at])

        def piece(p):
            @pl.when((p == 2) & (d >= 2) & (d < 4))
            def _():
                pair(2 * d - 4)

            ag_copy(own.at[p], odd, p, sgn).wait_recv()

            @pl.when(d < 4)
            def _():
                ag_copy(blk.at[odd - 1, p], odd + 2, p, sgn).start()

            pick(odd, p, blk.at[odd - 1, p])
            send(odd, p)

            @pl.when(d < 4)
            def _():
                ag_copy(own.at[p], even, p, -sgn).wait_recv()

                @pl.when(d < 3)
                def _():
                    ag_copy(blk.at[even - 1, p], even + 2, p, -sgn).start()

                pick(even, p, blk.at[even - 1, p])
                send(even, p)

        loop(0, 4, piece)

        @pl.when(d == 3)
        def _():
            far_copy().wait_recv()
            ovf32[0, 56:64, :] = far_in[...].astype(F32)[0:8]
            ovf32[1, 56:64, :] = far_in[...].astype(F32)[8:16]
            where_of = c64 == (r128 % 8) * 8 + r128 // 16
            first, second = mask((r128 % 16 < 8) & where_of), mask((r128 % 16 >= 8) & where_of)

            for n in (0, 1):
                a, b = ovf32[0, :, wide(n)].astype(BF), ovf32[1, :, wide(n)].astype(BF)
                ovsend[:, wide(n)] = (dot(first, a) + dot(second, b)).astype(BF)
            loop(1, 8, lambda i: over_copy(i).start())
            ovrecv[rows16(s * 16, 16), :] = ovsend[rows16(s * 16, 16), :]


    loop(1, 5, turn)

    pair(4)
    await_rows(6)
    loop(1, 8, lambda i: over_copy(i).wait_recv())
    take_lo = mask(c128 == (r64 // 8) * 16 + r64 % 8)
    take_hi = mask(c128 == (r64 // 8) * 16 + 8 + r64 % 8)

    for n in (0, 1):
        got = ovrecv[:, wide(n)]
        xs[0, OVER : OVER + COL * NZ, wide(n)] = dot(take_lo, got).astype(BF)
        xs[1, OVER : OVER + COL * NZ, wide(n)] = dot(take_hi, got).astype(BF)
    expert(
        6 * MAIN,
        MAIN + COL * NZ,
        [(0, 2, lambda n: (n * 64, 48 + s)), (2, 3, lambda n: (n * 64, 64 + s))],
    )

    put_lo = mask((r128 % 16 < 8) & (c64 == (r128 // 16) * 8 + r128 % 16))
    put_hi = mask((r128 % 16 >= 8) & (c64 == (r128 // 16) * 8 + r128 % 16 - 8))
    over_rows = pl.ds(OVER, COL * NZ)

    retov[...] = (dot(put_lo, retbuf[over_rows, wide(0)]) + dot(put_hi, retbuf[over_rows, wide(1)])).astype(BF)
    loop(1, 8, lambda i: back_over_copy(i).start())
    retovr[rows16(s * 16, 16), :] = retov[rows16(s * 16, 16), :]

    def send_back(pos):
        for i in range(1, 8):
            back_copy(pos, i).start()
        retrecv[pos, rows16(s * SLOT, SLOT), :] = retbuf[rows16(base(pos) + s * SLOT, SLOT), :]

    send_back(6)
    await_half(7, 0)
    expert(base(7), MAIN, [(0, 2, lambda n: (n * 64, 56 + s))], lambda: await_half(7, 1))
    send_back(7)
    for t in range(8):
        qbuf[t * 16 : t * 16 + 8, :] = qbuf[t * 16 : t * 16 + 8, :] + qbuf[MAIN + t * 8 : MAIN + t * 8 + 8, :]
    loop(1, 8, lambda i: q_copy(i).start())
    qin[rows16(s * 16, 16), :] = qbuf[rows16(s * 16, 16), :]

    def send_pair(k):
        send_back(4 - 2 * k)
        send_back(5 - 2 * k)

    loop(0, 2, send_pair)
    send_back(1)
    send_back(0)

    def weight_grad(j, m, emit):
        cols = pl.ds(pl.multiple_of(j * 512 + m * CW, CW), CW)
        emit(dot_tn(xs[0, :, cols], dgu[...]), dot_tn(xs[1, :, cols], hbuf[...]))

    def first_grads(m):
        def emit_to(slot):
            def emit(a, b):
                gsend[slot, tile(m), 0 : 2 * FF] = a.astype(BF)
                gsend[slot, tile(m), 2 * FF :] = b.astype(BF)

            return emit

        weight_grad((x + 2) % 4, m, emit_to(0))
        grad_copy(0, m, sgn).start()
        weight_grad((x - sgn + 4) % 4, m, emit_to(1))
        grad_copy(1, m, -sgn).start()

    loop(0, 2, first_grads)

    def own_grads(m):
        def emit(a, b):
            out_gu[tile(m), :] = a
            out_dn[tile(m), :] = b

        weight_grad(x, m, emit)

    loop(0, 2, own_grads)

    loop(1, 8, lambda i: back_over_copy(i).wait_recv())

    got_back = retovr[...]
    rovf[0:64, wide(0)] = dot(take_lo, got_back).astype(BF)
    rovf[0:64, wide(1)] = dot(take_hi, got_back).astype(BF)
    rovf[64:128, :] = jnp.zeros((64, D), BF)

    def combine(pos):
        for i in range(1, 8):
            back_copy(pos, i).wait_recv()

        for n in (0, 1):
            tf[:, wide(n)] = dot(sel_t[pos], retrecv[pos, :, wide(n)]) + dot(sov_t[pos], rovf[:, wide(n)])

    def pass_on(pos, k, has_more):
        combine(pos)
        for i in range(1, 8):
            back_copy(pos, i).wait_send()

        def piece(h):
            @pl.when(has_more)
            def _():
                sum_copy(pos + 2, h, k).wait_recv()

                def part(n):
                    at = rows16(h * 64 + n * 16, 16)
                    total = tf[at, :] + rsr[pos + 1, at, :].astype(F32)
                    retbuf[rows16(base(pos) + h * 64 + n * 16, 16), :] = total.astype(BF)

                loop(0, 4, part)

            @pl.when(jnp.logical_not(has_more))
            def _():
                def part(n):
                    at = rows16(h * 64 + n * 16, 16)
                    retbuf[rows16(base(pos) + h * 64 + n * 16, 16), :] = tf[at, :].astype(BF)

                loop(0, 4, part)

            sum_copy(pos, h, k).start()

        loop(0, 2, piece)

    def add_grads(slot):
        def part(n):
            at = rows16(n * 32, 32)
            more = grecv[slot, at, :].astype(F32)
            out_gu[at, :] = out_gu[at, :] + more[:, 0 : 2 * FF]
            out_dn[at, :] = out_dn[at, :] + more[:, 2 * FF :]

        loop(0, 512 // 32, part)

    def drain():
        far_copy().wait_send()
        loop(1, 8, lambda i: meta_copy(i).wait_send())
        loop(1, 8, lambda i: over_copy(i).wait_send())
        loop(1, 8, lambda i: back_over_copy(i).wait_send())

        def drain_rows(pos):
            loop(0, 4, lambda p: loop(1, 8, lambda i: row_copy(pos, p, i).wait_send()))

        loop(0, NZ, drain_rows)

        def drain_ring(pos):
            for p in range(4):
                ag_copy(own.at[p], pos, p, sgn).wait_send()

        loop(1, 8, drain_ring)

    def routers():
        loop(1, 8, lambda i: q_copy(i).wait_recv())
        held = qin[0:16, :]
        for o in range(1, 8):
            held = held + qin[o * 16 : o * 16 + 16, :]
        for pos in range(NZ):
            one = sel[0, pos, :, :].astype(F32)
            rows = []
            for o in range(8):
                value = held[:, pos * 8 + o : pos * 8 + o + 1]
                row = jnp.sum(one[o * 16 : o * 16 + 16] * value, axis=0, keepdims=True)
                rows.append(row + one[MAIN + o : MAIN + o + 1] * held[pos : pos + 1, 64 + o : 65 + o])
            gq[pos] = jnp.concatenate(rows, axis=0)
        for pos in range(1, NZ):
            p_copy(pos).start()
        gall[z] = gq[0]

    def back_turn(k):
        @pl.when(k < 3)
        def _():
            pass_on(6 - 2 * k, sgn, k > 0)

        pass_on(7 - 2 * k, -sgn, k > 0)

        @pl.when(k < 2)
        def _():
            m = k
            grad_copy(0, m, sgn).wait()

            def emit(a, b):
                got = grecv[0, tile(m), :].astype(F32)
                gsend[0, tile(m), 0 : 2 * FF] = (a + got[:, 0 : 2 * FF]).astype(BF)
                gsend[0, tile(m), 2 * FF :] = (b + got[:, 2 * FF :]).astype(BF)

            weight_grad((x + sgn + 4) % 4, m, emit)
            grad_copy(2, m, sgn).start()

        @pl.when(k == 0)
        def _():
            routers()

        @pl.when(k == 1)
        def _():
            drain()

        @pl.when(k == 2)
        def _():
            for m in (0, 1):
                grad_copy(1, m, -sgn).wait()
            add_grads(1)

    loop(0, 4, back_turn)

    for m in (0, 1):
        grad_copy(2, m, sgn).wait()
    add_grads(2)
    gu_out = pltpu.make_async_copy(out_gu, gu_hbm, w_sem.at[0])
    dn_out = pltpu.make_async_copy(out_dn, dn_hbm, w_sem.at[1])
    gu_out.start()
    dn_out.start()

    for pos in range(1, NZ):
        p_copy(pos).wait()
    by_lane = gall[...].reshape(64, TOK)
    rows = []
    for k in range(8):
        hit = ids_t[k : k + 1, :] == lane_of
        rows.append(jnp.sum(jnp.where(hit, by_lane, 0.0), axis=0, keepdims=True))
    out_prob[...] = (jnp.concatenate(rows, axis=0) / probs_t).astype(BF)

    combine(0)
    for pos in (1, 2):
        for h in (0, 1):
            sum_copy(pos, h, sgn).wait_recv()

    def finish(n):
        at = rows16(n * 16, 16)
        total = tf[at, :] + rsr[0, at, :].astype(F32) + rsr[1, at, :].astype(F32)
        out_tok[at, :] = total.astype(BF)

    loop(0, TOK // 16, finish)
    loop(1, 8, lambda i: back_copy(0, i).wait_send())
    loop(1, 8, lambda i: q_copy(i).wait_send())

    def drain_sums(pos):
        sum_copy(pos, 0, sgn).wait_send()
        sum_copy(pos, 1, sgn).wait_send()

    loop(1, 8, drain_sums)
    gu_out.wait()
    dn_out.wait()


def copy_out(*refs):
    sources, targets, held, sems = refs[:4], refs[4:8], refs[8:12], refs[12]
    parts = [(0, 0, 128), (1, 0, 8)] + [(2, k * 128, 128) for k in range(4)] + [(3, k * 256, 256) for k in range(2)]

    def copy(at, which, a, b):
        n, start, count = parts[at]
        rows = pl.ds(start, count)
        return pltpu.make_async_copy(a[n].at[rows], b[n].at[rows], sems.at[which, at])

    for at in range(len(parts)):
        copy(at, 0, sources, held).start()
    for at in range(len(parts)):
        copy(at, 0, sources, held).wait()
        copy(at, 1, held, targets).start()
    for at in range(len(parts)):
        copy(at, 1, held, targets).wait()


def on_device(tokens, out_grad, expert_ids, route_probs, w_gate_up, w_down):
    vm, dma = pltpu.VMEM, pltpu.SemaphoreType.DMA
    inside = pl.BlockSpec(memory_space=pltpu.VMEM)
    token_grad, prob_grad, grad_gu, grad_dn = pl.pallas_call(
        kernel,
        out_shape=(
            jax.ShapeDtypeStruct((TOK, D), BF),
            jax.ShapeDtypeStruct((8, TOK), BF),
            jax.ShapeDtypeStruct((512, 2 * FF), F32),
            jax.ShapeDtypeStruct((512, FF), F32),
        ),
        in_specs=[pl.BlockSpec(memory_space=pl.ANY)] * 2 + [inside] * 2 + [pl.BlockSpec(memory_space=pl.ANY)] * 2,
        out_specs=(inside,) * 2 + (pl.BlockSpec(memory_space=pl.ANY),) * 2,
        scratch_shapes=[
            vm((512, 2 * FF), F32),
            vm((512, FF), F32),
            vm((4, TOK, D // 2), BF),
            vm((D, 2 * FF), BF),
            vm((D, FF), BF),
            vm((NZ, 16, TOK), F32),
            vm((NZ, 16, TOK), F32),
            vm((16, D), BF),
            vm((16, D), BF),
            vm((2, NZ, MAIN + 16, TOK), BF),
            vm((NZ, TOK, MAIN), BF),
            vm((NZ, TOK, 128), BF),
            vm((NZ - 1, 4, TOK, D // 2), BF),
            vm((NZ, 4, MAIN, D // 2), BF),
            vm((2, 64, D), F32),
            vm((128, D), BF),
            vm((128, D), BF),
            vm((2, ROWS, D), BF),
            vm((320, 2 * FF), F32),
            vm((320, FF), F32),
            vm((ROWS, FF), BF),
            vm((ROWS, 2 * FF), BF),
            vm((ROWS, D), BF),
            vm((NZ, MAIN, D), BF),
            vm((128, D // 2), BF),
            vm((128, D // 2), BF),
            vm((128, D), BF),
            vm((TOK, D), F32),
            vm((NZ - 1, TOK, D), BF),
            vm((2, 512, 3 * FF), BF),
            vm((3, 512, 3 * FF), BF),
            vm((192, 128), F32),
            vm((128, 128), F32),
            vm((NZ, 8, TOK), F32),
            vm((NZ, 8, TOK), F32),
            dma((6,)),
            dma((2,)),
            dma((8,)), dma((8,)),
            dma((7, 4)), dma((7, 4)),
            dma((32, 8)), dma((32, 8)),
            dma((8,)), dma((8,)),
            dma((8, 8)), dma((8, 8)),
            dma((8,)), dma((8,)),
            dma((7, 2)), dma((7, 2)),
            dma((3, 2)), dma((3, 2)),
            dma((8,)), dma((8,)),
            dma((8,)), dma((8,)),
        ],
        compiler_params=pltpu.CompilerParams(
            collective_id=0, has_side_effects=True, vmem_limit_bytes=62 * 2**20
        ),
        cost_estimate=pl.CostEstimate(flops=15 * 10**9, bytes_accessed=10**7, transcendentals=10**6),
        name="routed_backward",
    )(tokens, out_grad, expert_ids.T, route_probs.T, w_gate_up[0], w_down[0])
    results = (token_grad, prob_grad, grad_gu, grad_dn)
    anywhere = pl.BlockSpec(memory_space=pltpu.HBM)
    token_grad, prob_grad, grad_gu, grad_dn = pl.pallas_call(
        copy_out,
        out_shape=tuple(jax.ShapeDtypeStruct(r.shape, r.dtype) for r in results),
        in_specs=[anywhere] * 4,
        out_specs=(anywhere,) * 4,
        scratch_shapes=[vm(r.shape, r.dtype) for r in results] + [dma((2, 8))],
        name="results",
    )(*results)
    return token_grad, prob_grad.T, grad_gu[None], grad_dn[None]


def solution(mesh):
    in_specs = (
        P(("expert", "dp"), None),
        P(("expert", "dp"), None),
        P(("expert", "dp"), None),
        P(("expert", "dp"), None),
        P("expert", None, None),
        P("expert", None, None),
    )
    out_specs = (
        P(("expert", "dp"), None),
        P(("expert", "dp"), None),
        P("expert", "dp", None),
        P("expert", "dp", None),
    )
    return jax.shard_map(
        on_device, mesh=mesh, in_specs=in_specs, out_specs=out_specs, check_vma=False
    )
```

```python
import functools

import jax
import jax.numpy as jnp
from jax import lax
from jax.experimental import pallas as pl
from jax.experimental.pallas import tpu as pltpu
from jax.sharding import PartitionSpec as P

MESH = pl.DeviceIdType.MESH
BF = jnp.bfloat16
F32 = jnp.float32

NZ = 8
COL = 8
TOK = 128
D = 2048
FF = 384
SLOT = 16
MAIN = COL * SLOT
ROWS = NZ * MAIN + COL * NZ
OVER = (NZ - 1) * MAIN
CW = 256


def iota(shape, dim):
    return lax.broadcasted_iota(jnp.int32, shape, dim)


def dot(a, b):
    return jnp.dot(a, b, preferred_element_type=F32)


def dot_nt(a, b):
    return lax.dot_general(a, b, (((1,), (1,)), ((), ())), preferred_element_type=F32)


def dot_tn(a, b):
    return lax.dot_general(a, b, (((0,), (0,)), ((), ())), preferred_element_type=F32)


def tile(n, width=CW):
    return pl.ds(pl.multiple_of(n * width, width), width)


def wide(n):
    return slice(n * 1024, n * 1024 + 1024)


def rows16(start, count):
    return pl.ds(pl.multiple_of(start, 16), count)


def mask(cond, dtype=BF):
    return jnp.where(cond, 1.0, 0.0).astype(dtype)


def kernel(
    tok_hbm, dy_hbm, ids_ref, probs_ref, wgu_hbm, wdn_hbm,
    out_tok, out_prob, gu_hbm, dn_hbm,
    out_gu, out_dn, own, wgu, wdn, meta_own, meta_all, far, far_in, sel, sel_t, sov_t, blk, sendbuf, ovf32, ovsend, ovrecv,
    xs, gu, hg, hbuf, dgu, retbuf, retrecv, retov, retovr, rovf, tf, rsr, gsend, grecv, qbuf, qin, gq, gall,
    w_sem, far_sem, meta_s, meta_r, ag_s, ag_r, d_s, d_r, ov_s, ov_r, r_s, r_r, ro_s, ro_r, rs_s, rs_r, g_s, g_r, q_s, q_r, p_s, p_r,
):
    e = lax.axis_index("expert")
    x = lax.axis_index("dp")
    y, z, c = e // 16, (e // 2) % 8, e % 2
    s = y * 2 + c
    sgn = 1 - 2 * c

    def zdev(k):
        return ((y * 8 + (z + k + 8) % 8) * 2 + c, x)

    def coldev(t):
        return (((t // 2) * 8 + z) * 2 + t % 2, x)

    other = [(s + i) % 8 for i in range(8)]
    other_dev = [coldev(t) for t in other]

    def xdev(k):
        return (e, (x + k + 4) % 4)

    def remote(src, dst, ss, rs, dev):
        return pltpu.make_async_remote_copy(
            src_ref=src, dst_ref=dst, send_sem=ss, recv_sem=rs, device_id=dev, device_id_type=MESH
        )

    def base(pos):
        return pos * MAIN + (pos // (NZ - 1)) * COL * NZ

    def loop(lo, hi, fn):
        def step(i, carry):
            fn(i)
            return carry

        lax.fori_loop(lo, hi, step, 0)

    def meta_copy(i):
        return remote(
            meta_own.at[(z + i) % 8], meta_all.at[i], meta_s.at[i], meta_r.at[i], zdev(i)
        )

    def ag_copy(src, pos, p, k):
        return remote(src, blk.at[pos - 1, p], ag_s.at[pos - 1, p], ag_r.at[pos - 1, p], zdev(k))

    def row_copy(pos, p, i):
        t, dev = (other[i], other_dev[i]) if isinstance(i, int) else (s, coldev((s + i) % 8))
        return remote(
            sendbuf.at[pos, p, rows16(t * SLOT, SLOT)],
            xs.at[p // 2, rows16(base(pos) + s * SLOT, SLOT), tile(p % 2, 1024)],
            d_s.at[pos * 4 + p, i],
            d_r.at[pos * 4 + p, i],
            dev,
        )

    def over_copy(i):
        t = (s + i) % 8
        return remote(
            ovsend.at[rows16(t * 16, 16)], ovrecv.at[rows16(s * 16, 16)], ov_s.at[i], ov_r.at[i], coldev(t)
        )

    def back_copy(pos, i):
        t, dev = (other[i], other_dev[i]) if isinstance(i, int) else (s, coldev((s + i) % 8))
        return remote(
            retbuf.at[rows16(base(pos) + t * SLOT, SLOT)],
            retrecv.at[pos, rows16(s * SLOT, SLOT)],
            r_s.at[pos, i],
            r_r.at[pos, i],
            dev,
        )

    def back_over_copy(i):
        t = (s + i) % 8
        return remote(
            retov.at[rows16(t * 16, 16)], retovr.at[rows16(s * 16, 16)], ro_s.at[i], ro_r.at[i], coldev(t)
        )

    def sum_copy(pos, piece, k):
        return remote(
            retbuf.at[rows16(base(pos) + piece * 64, 64)],
            rsr.at[pos - 1, rows16(piece * 64, 64)],
            rs_s.at[pos - 1, piece],
            rs_r.at[pos - 1, piece],
            zdev(k),
        )

    def grad_copy(slot, half, k):
        return remote(
            gsend.at[slot % 2, tile(half)],
            grecv.at[slot, tile(half)],
            g_s.at[slot, half],
            g_r.at[slot, half],
            xdev(k),
        )

    def q_copy(i):
        t = (s + i) % 8
        return remote(qbuf.at[rows16(t * 16, 16)], qin.at[rows16(s * 16, 16)], q_s.at[i], q_r.at[i], coldev(t))

    def p_copy(pos):
        k = -sgn * ((pos + 1) // 2) if pos % 2 else sgn * (pos // 2)
        return remote(gq.at[pos], gall.at[z], p_s.at[pos], p_r.at[pos], zdev(k))

    def far_copy():
        return remote(far, far_in, far_sem.at[0], far_sem.at[1], zdev(4))

    barrier = pltpu.get_barrier_semaphore()
    for i in range(1, 8):
        pl.semaphore_signal(barrier, inc=1, device_id=zdev(i), device_id_type=MESH)
        pl.semaphore_signal(barrier, inc=1, device_id=coldev((s + i) % 8), device_id_type=MESH)
    for k in (-1, 1):
        pl.semaphore_signal(barrier, inc=1, device_id=xdev(k), device_id_type=MESH)
    own_copies = [
        pltpu.make_async_copy((tok_hbm, tok_hbm, dy_hbm, dy_hbm)[p].at[:, wide(p % 2)], own.at[p], w_sem.at[2 + p])
        for p in range(4)
    ]
    for one_copy in own_copies:
        one_copy.start()
    w_gu_copy = pltpu.make_async_copy(wgu_hbm, wgu, w_sem.at[0])
    w_dn_copy = pltpu.make_async_copy(wdn_hbm, wdn, w_sem.at[1])
    w_gu_copy.start()
    w_dn_copy.start()
    qbuf[...] = jnp.zeros((192, 128), F32)

    def by_z(ids):
        return ((ids // 2) % 8) * 8 + (ids // 16) * 2 + ids % 2

    ids_t = by_z(ids_ref[...])
    probs_t = probs_ref[...].astype(F32)
    lane_of = iota((64, TOK), 0)
    named = jnp.zeros((64, TOK), F32)
    weight = jnp.zeros((64, TOK), F32)
    for k in range(8):
        hit = ids_t[k : k + 1, :] == lane_of
        named += jnp.where(hit, 1.0, 0.0)
        weight += jnp.where(hit, probs_t[k : k + 1, :], 0.0)
    before = mask(iota((TOK, TOK), 0) < iota((TOK, TOK), 1))
    rank = jnp.where(named > 0.0, dot(named.astype(BF), before), -1.0)
    for k in range(NZ):
        meta_own[k, 0:8, :] = rank[k * 8 : k * 8 + 8]
        meta_own[k, 8:16, :] = weight[k * 8 : k * 8 + 8]

    def build(pos, info):
        ranks, weights = info[0:8], info[8:16]

        def spread(a, n):
            return jnp.concatenate([jnp.broadcast_to(a[k : k + 1], (n, TOK)) for k in range(8)], axis=0)

        hit = spread(ranks, SLOT) == (iota((MAIN, TOK), 0) % SLOT).astype(F32)
        over = ranks == float(SLOT)
        none = jnp.zeros((8, TOK), F32)
        one = jnp.where(hit, 1.0, 0.0)
        sel[0, pos, 0:MAIN, :] = one.astype(BF)
        sel[0, pos, MAIN : MAIN + 16, :] = jnp.concatenate([jnp.where(over, 1.0, 0.0), none], axis=0).astype(BF)
        sel[1, pos, 0:MAIN, :] = jnp.where(hit, spread(weights, SLOT), 0.0).astype(BF)
        sel[1, pos, MAIN : MAIN + 16, :] = jnp.concatenate([jnp.where(over, weights, 0.0), none], axis=0).astype(BF)
        sel_t[pos] = one.T.astype(BF)
        mine = (spread(ranks, 8) == float(SLOT)) & (iota((64, TOK), 0) % 8 == pos)
        wide = jnp.concatenate([jnp.where(mine, 1.0, 0.0), jnp.zeros((64, TOK), F32)], axis=0)
        sov_t[pos] = wide.T.astype(BF)

    def pick(pos, p, ref):
        got = dot(sel[p // 2, pos], ref[...])
        sendbuf[pos, p] = got[:MAIN].astype(BF)
        ovf32[p // 2, pl.ds(pl.multiple_of(pos * 8, 8), 8), tile(p % 2, 1024)] = got[MAIN : MAIN + 8]

    def send(pos, p):
        for i in range(1, 8):
            row_copy(pos, p, i).start()
        xs[p // 2, rows16(base(pos) + s * SLOT, SLOT), tile(p % 2, 1024)] = sendbuf[pos, p, rows16(s * SLOT, SLOT), :]

    def await_half(pos, p):
        for i in range(1, 8):
            row_copy(pos, 2 * p, i).wait_recv()
            row_copy(pos, 2 * p + 1, i).wait_recv()

    def await_rows(pos):
        await_half(pos, 0)
        await_half(pos, 1)

    def expert(row0, count, places, between=lambda: None):
        rows = rows16(row0, count)
        gu[0:count, :] = dot(xs[0, rows, :], wgu[...])
        between()
        hg[0:count, :] = dot(xs[1, rows, :], wdn[...])

        def middle(n, place, lane):
            part, whole = rows16(n * 64, 64), rows16(row0 + n * 64, 64)
            gate, up, grad = gu[part, 0:FF], gu[part, FF : 2 * FF], hg[part, :]
            sig = jax.nn.sigmoid(gate)
            silu = gate * sig
            act = (silu * up).astype(BF)
            hbuf[whole, :] = act
            dgu[whole, 0:FF] = (grad * up * sig * (1.0 + gate * (1.0 - sig))).astype(BF)
            dgu[whole, FF : 2 * FF] = (grad * silu).astype(BF)
            router = jnp.sum(grad * act.astype(F32), axis=1, keepdims=True)
            at = pl.ds(pl.multiple_of(place, 16), 64)
            qbuf[at, :] = qbuf[at, :] + jnp.where(iota((64, 128), 1) == lane, router, 0.0)

        for lo, hi, place in places:
            loop(lo, hi, lambda n, place=place: middle(n, *place(n)))

        def last(n):
            retbuf[rows, tile(n, 512)] = dot_nt(dgu[rows, :], wgu[tile(n, 512), :]).astype(BF)

        loop(0, D // 512, last)

    build(0, meta_own[z])
    own_copies[0].wait()
    pick(0, 0, own.at[0])

    pl.semaphore_wait(barrier, 16)

    def own_ring(p):
        ag_copy(own.at[p], 1, p, sgn).start()
        ag_copy(own.at[p], 2, p, -sgn).start()

    loop(1, 8, lambda i: meta_copy(i).start())
    own_ring(0)
    send(0, 0)
    for p in (1, 2, 3):
        own_copies[p].wait()
        own_ring(p)
    for p in (1, 2, 3):
        pick(0, p, own.at[p])
        send(0, p)

    opposite = meta_own[(z + 4) % 8]
    nobody = jnp.zeros((8, TOK), F32)
    far_one = jnp.concatenate([jnp.where(opposite[0:8] == float(SLOT), 1.0, 0.0), nobody], axis=0).astype(BF)
    far_weight = jnp.concatenate([nobody, jnp.where(opposite[0:8] == float(SLOT), opposite[8:16], 0.0)], axis=0).astype(BF)

    for n in (0, 1):
        far[:, wide(n)] = (dot(far_one, own[n]) + dot(far_weight, own[2 + n])).astype(BF)
    far_copy().start()
    w_gu_copy.wait()
    w_dn_copy.wait()

    r128, c64 = iota((128, 64), 0), iota((128, 64), 1)
    r64, c128 = iota((64, 128), 0), iota((64, 128), 1)

    def pair(pos):
        await_rows(pos)
        await_rows(pos + 1)
        expert(pos * MAIN, 2 * MAIN, [(0, 4, lambda n: ((n % 2) * 64, (pos + n // 2) * 8 + s))])

    def turn(d):
        odd, even = 2 * d - 1, 2 * d
        up_at, down_at = (8 + sgn * d) % 8, (8 - sgn * d) % 8
        meta_copy(up_at).wait_recv()
        build(odd, meta_all[up_at])

        @pl.when(d < 4)
        def _():
            meta_copy(down_at).wait_recv()
            build(even, meta_all[down_at])

        def piece(p):
            @pl.when((p == 2) & (d >= 2) & (d < 4))
            def _():
                pair(2 * d - 4)

            ag_copy(own.at[p], odd, p, sgn).wait_recv()

            @pl.when(d < 4)
            def _():
                ag_copy(blk.at[odd - 1, p], odd + 2, p, sgn).start()

            pick(odd, p, blk.at[odd - 1, p])
            send(odd, p)

            @pl.when(d < 4)
            def _():
                ag_copy(own.at[p], even, p, -sgn).wait_recv()

                @pl.when(d < 3)
                def _():
                    ag_copy(blk.at[even - 1, p], even + 2, p, -sgn).start()

                pick(even, p, blk.at[even - 1, p])
                send(even, p)

        loop(0, 4, piece)

        @pl.when(d == 3)
        def _():
            far_copy().wait_recv()
            ovf32[0, 56:64, :] = far_in[...].astype(F32)[0:8]
            ovf32[1, 56:64, :] = far_in[...].astype(F32)[8:16]
            where_of = c64 == (r128 % 8) * 8 + r128 // 16
            first, second = mask((r128 % 16 < 8) & where_of), mask((r128 % 16 >= 8) & where_of)

            for n in (0, 1):
                a, b = ovf32[0, :, wide(n)].astype(BF), ovf32[1, :, wide(n)].astype(BF)
                ovsend[:, wide(n)] = (dot(first, a) + dot(second, b)).astype(BF)
            loop(1, 8, lambda i: over_copy(i).start())
            ovrecv[rows16(s * 16, 16), :] = ovsend[rows16(s * 16, 16), :]


    loop(1, 5, turn)

    pair(4)
    await_rows(6)
    loop(1, 8, lambda i: over_copy(i).wait_recv())
    take_lo = mask(c128 == (r64 // 8) * 16 + r64 % 8)
    take_hi = mask(c128 == (r64 // 8) * 16 + 8 + r64 % 8)

    for n in (0, 1):
        got = ovrecv[:, wide(n)]
        xs[0, OVER : OVER + COL * NZ, wide(n)] = dot(take_lo, got).astype(BF)
        xs[1, OVER : OVER + COL * NZ, wide(n)] = dot(take_hi, got).astype(BF)
    expert(
        6 * MAIN,
        MAIN + COL * NZ,
        [(0, 2, lambda n: (n * 64, 48 + s)), (2, 3, lambda n: (n * 64, 64 + s))],
    )

    put_lo = mask((r128 % 16 < 8) & (c64 == (r128 // 16) * 8 + r128 % 16))
    put_hi = mask((r128 % 16 >= 8) & (c64 == (r128 // 16) * 8 + r128 % 16 - 8))
    over_rows = pl.ds(OVER, COL * NZ)

    retov[...] = (dot(put_lo, retbuf[over_rows, wide(0)]) + dot(put_hi, retbuf[over_rows, wide(1)])).astype(BF)
    loop(1, 8, lambda i: back_over_copy(i).start())
    retovr[rows16(s * 16, 16), :] = retov[rows16(s * 16, 16), :]

    def send_back(pos):
        for i in range(1, 8):
            back_copy(pos, i).start()
        retrecv[pos, rows16(s * SLOT, SLOT), :] = retbuf[rows16(base(pos) + s * SLOT, SLOT), :]

    send_back(6)
    await_half(7, 0)
    expert(base(7), MAIN, [(0, 2, lambda n: (n * 64, 56 + s))], lambda: await_half(7, 1))
    send_back(7)
    for t in range(8):
        qbuf[t * 16 : t * 16 + 8, :] = qbuf[t * 16 : t * 16 + 8, :] + qbuf[MAIN + t * 8 : MAIN + t * 8 + 8, :]
    loop(1, 8, lambda i: q_copy(i).start())
    qin[rows16(s * 16, 16), :] = qbuf[rows16(s * 16, 16), :]

    def send_pair(k):
        send_back(5 - 2 * k)
        send_back(4 - 2 * k)

    loop(0, 2, send_pair)
    send_back(1)
    send_back(0)

    def weight_grad(j, m, emit):
        cols = pl.ds(pl.multiple_of(j * 512 + m * CW, CW), CW)
        emit(dot_tn(xs[0, :, cols], dgu[...]), dot_tn(xs[1, :, cols], hbuf[...]))

    def first_grads(m):
        def emit_to(slot):
            def emit(a, b):
                gsend[slot, tile(m), 0 : 2 * FF] = a.astype(BF)
                gsend[slot, tile(m), 2 * FF :] = b.astype(BF)

            return emit

        weight_grad((x + 2) % 4, m, emit_to(0))
        grad_copy(0, m, sgn).start()
        weight_grad((x - sgn + 4) % 4, m, emit_to(1))
        grad_copy(1, m, -sgn).start()

    loop(0, 2, first_grads)

    def own_grads(m):
        def emit(a, b):
            out_gu[tile(m), :] = a
            out_dn[tile(m), :] = b

        weight_grad(x, m, emit)

    loop(0, 2, own_grads)

    loop(1, 8, lambda i: back_over_copy(i).wait_recv())

    got_back = retovr[...]
    rovf[0:64, wide(0)] = dot(take_lo, got_back).astype(BF)
    rovf[0:64, wide(1)] = dot(take_hi, got_back).astype(BF)
    rovf[64:128, :] = jnp.zeros((64, D), BF)

    def combine(pos):
        for i in range(1, 8):
            back_copy(pos, i).wait_recv()

        for n in (0, 1):
            tf[:, wide(n)] = dot(sel_t[pos], retrecv[pos, :, wide(n)]) + dot(sov_t[pos], rovf[:, wide(n)])

    def pass_on(pos, k, has_more):
        combine(pos)
        for i in range(1, 8):
            back_copy(pos, i).wait_send()

        def piece(h):
            @pl.when(has_more)
            def _():
                sum_copy(pos + 2, h, k).wait_recv()

                def part(n):
                    at = rows16(h * 64 + n * 16, 16)
                    total = tf[at, :] + rsr[pos + 1, at, :].astype(F32)
                    retbuf[rows16(base(pos) + h * 64 + n * 16, 16), :] = total.astype(BF)

                loop(0, 4, part)

            @pl.when(jnp.logical_not(has_more))
            def _():
                def part(n):
                    at = rows16(h * 64 + n * 16, 16)
                    retbuf[rows16(base(pos) + h * 64 + n * 16, 16), :] = tf[at, :].astype(BF)

                loop(0, 4, part)

            sum_copy(pos, h, k).start()

        loop(0, 2, piece)

    def add_grads(slot):
        def part(n):
            at = rows16(n * 32, 32)
            more = grecv[slot, at, :].astype(F32)
            out_gu[at, :] = out_gu[at, :] + more[:, 0 : 2 * FF]
            out_dn[at, :] = out_dn[at, :] + more[:, 2 * FF :]

        loop(0, 512 // 32, part)

    def drain():
        far_copy().wait_send()
        loop(1, 8, lambda i: meta_copy(i).wait_send())
        loop(1, 8, lambda i: over_copy(i).wait_send())
        loop(1, 8, lambda i: back_over_copy(i).wait_send())

        def drain_rows(pos):
            loop(0, 4, lambda p: loop(1, 8, lambda i: row_copy(pos, p, i).wait_send()))

        loop(0, NZ, drain_rows)

        def drain_ring(pos):
            for p in range(4):
                ag_copy(own.at[p], pos, p, sgn).wait_send()

        loop(1, 8, drain_ring)

    def routers():
        loop(1, 8, lambda i: q_copy(i).wait_recv())
        held = qin[0:16, :]
        for o in range(1, 8):
            held = held + qin[o * 16 : o * 16 + 16, :]
        for pos in range(NZ):
            one = sel[0, pos, :, :].astype(F32)
            rows = []
            for o in range(8):
                value = held[:, pos * 8 + o : pos * 8 + o + 1]
                row = jnp.sum(one[o * 16 : o * 16 + 16] * value, axis=0, keepdims=True)
                rows.append(row + one[MAIN + o : MAIN + o + 1] * held[pos : pos + 1, 64 + o : 65 + o])
            gq[pos] = jnp.concatenate(rows, axis=0)
        for pos in range(1, NZ):
            p_copy(pos).start()
        gall[z] = gq[0]

    def back_turn(k):
        @pl.when(k == 0)
        def _():
            pass_on(6, sgn, k > 0)

        pass_on(7 - 2 * k, -sgn, k > 0)

        @pl.when((k == 1) | (k == 2))
        def _():
            pass_on(6 - 2 * k, sgn, k > 0)
            m = k - 1
            grad_copy(0, m, sgn).wait()

            def emit(a, b):
                got = grecv[0, tile(m), :].astype(F32)
                gsend[0, tile(m), 0 : 2 * FF] = (a + got[:, 0 : 2 * FF]).astype(BF)
                gsend[0, tile(m), 2 * FF :] = (b + got[:, 2 * FF :]).astype(BF)

            weight_grad((x + sgn + 4) % 4, m, emit)
            grad_copy(2, m, sgn).start()

        @pl.when(k == 0)
        def _():
            routers()

        @pl.when(k == 1)
        def _():
            drain()

        @pl.when(k == 2)
        def _():
            for m in (0, 1):
                grad_copy(1, m, -sgn).wait()
            add_grads(1)

    loop(0, 4, back_turn)

    for m in (0, 1):
        grad_copy(2, m, sgn).wait()
    add_grads(2)
    gu_out = pltpu.make_async_copy(out_gu, gu_hbm, w_sem.at[0])
    dn_out = pltpu.make_async_copy(out_dn, dn_hbm, w_sem.at[1])
    gu_out.start()
    dn_out.start()

    for pos in range(1, NZ):
        p_copy(pos).wait()
    by_lane = gall[...].reshape(64, TOK)
    rows = []
    for k in range(8):
        hit = ids_t[k : k + 1, :] == lane_of
        rows.append(jnp.sum(jnp.where(hit, by_lane, 0.0), axis=0, keepdims=True))
    out_prob[...] = (jnp.concatenate(rows, axis=0) / probs_t).astype(BF)

    combine(0)
    for pos in (1, 2):
        for h in (0, 1):
            sum_copy(pos, h, sgn).wait_recv()

    def finish(n):
        at = rows16(n * 16, 16)
        total = tf[at, :] + rsr[0, at, :].astype(F32) + rsr[1, at, :].astype(F32)
        out_tok[at, :] = total.astype(BF)

    loop(0, TOK // 16, finish)
    loop(1, 8, lambda i: back_copy(0, i).wait_send())
    loop(1, 8, lambda i: q_copy(i).wait_send())

    def drain_sums(pos):
        sum_copy(pos, 0, sgn).wait_send()
        sum_copy(pos, 1, sgn).wait_send()

    loop(1, 8, drain_sums)
    gu_out.wait()
    dn_out.wait()


def copy_out(*refs):
    sources, targets, held, sems = refs[:4], refs[4:8], refs[8:12], refs[12]
    parts = [(0, 0, 128), (1, 0, 8)] + [(2, k * 128, 128) for k in range(4)] + [(3, k * 256, 256) for k in range(2)]

    def copy(at, which, a, b):
        n, start, count = parts[at]
        rows = pl.ds(start, count)
        return pltpu.make_async_copy(a[n].at[rows], b[n].at[rows], sems.at[which, at])

    for at in range(len(parts)):
        copy(at, 0, sources, held).start()
    for at in range(len(parts)):
        copy(at, 0, sources, held).wait()
        copy(at, 1, held, targets).start()
    for at in range(len(parts)):
        copy(at, 1, held, targets).wait()


def on_device(tokens, out_grad, expert_ids, route_probs, w_gate_up, w_down):
    vm, dma = pltpu.VMEM, pltpu.SemaphoreType.DMA
    inside = pl.BlockSpec(memory_space=pltpu.VMEM)
    token_grad, prob_grad, grad_gu, grad_dn = pl.pallas_call(
        kernel,
        out_shape=(
            jax.ShapeDtypeStruct((TOK, D), BF),
            jax.ShapeDtypeStruct((8, TOK), BF),
            jax.ShapeDtypeStruct((512, 2 * FF), F32),
            jax.ShapeDtypeStruct((512, FF), F32),
        ),
        in_specs=[pl.BlockSpec(memory_space=pl.ANY)] * 2 + [inside] * 2 + [pl.BlockSpec(memory_space=pl.ANY)] * 2,
        out_specs=(inside,) * 2 + (pl.BlockSpec(memory_space=pl.ANY),) * 2,
        scratch_shapes=[
            vm((512, 2 * FF), F32),
            vm((512, FF), F32),
            vm((4, TOK, D // 2), BF),
            vm((D, 2 * FF), BF),
            vm((D, FF), BF),
            vm((NZ, 16, TOK), F32),
            vm((NZ, 16, TOK), F32),
            vm((16, D), BF),
            vm((16, D), BF),
            vm((2, NZ, MAIN + 16, TOK), BF),
            vm((NZ, TOK, MAIN), BF),
            vm((NZ, TOK, 128), BF),
            vm((NZ - 1, 4, TOK, D // 2), BF),
            vm((NZ, 4, MAIN, D // 2), BF),
            vm((2, 64, D), F32),
            vm((128, D), BF),
            vm((128, D), BF),
            vm((2, ROWS, D), BF),
            vm((320, 2 * FF), F32),
            vm((320, FF), F32),
            vm((ROWS, FF), BF),
            vm((ROWS, 2 * FF), BF),
            vm((ROWS, D), BF),
            vm((NZ, MAIN, D), BF),
            vm((128, D // 2), BF),
            vm((128, D // 2), BF),
            vm((128, D), BF),
            vm((TOK, D), F32),
            vm((NZ - 1, TOK, D), BF),
            vm((2, 512, 3 * FF), BF),
            vm((3, 512, 3 * FF), BF),
            vm((192, 128), F32),
            vm((128, 128), F32),
            vm((NZ, 8, TOK), F32),
            vm((NZ, 8, TOK), F32),
            dma((6,)),
            dma((2,)),
            dma((8,)), dma((8,)),
            dma((7, 4)), dma((7, 4)),
            dma((32, 8)), dma((32, 8)),
            dma((8,)), dma((8,)),
            dma((8, 8)), dma((8, 8)),
            dma((8,)), dma((8,)),
            dma((7, 2)), dma((7, 2)),
            dma((3, 2)), dma((3, 2)),
            dma((8,)), dma((8,)),
            dma((8,)), dma((8,)),
        ],
        compiler_params=pltpu.CompilerParams(
            collective_id=0, has_side_effects=True, vmem_limit_bytes=62 * 2**20
        ),
        cost_estimate=pl.CostEstimate(flops=15 * 10**9, bytes_accessed=10**7, transcendentals=10**6),
        name="routed_backward",
    )(tokens, out_grad, expert_ids.T, route_probs.T, w_gate_up[0], w_down[0])
    results = (token_grad, prob_grad, grad_gu, grad_dn)
    anywhere = pl.BlockSpec(memory_space=pltpu.HBM)
    token_grad, prob_grad, grad_gu, grad_dn = pl.pallas_call(
        copy_out,
        out_shape=tuple(jax.ShapeDtypeStruct(r.shape, r.dtype) for r in results),
        in_specs=[anywhere] * 4,
        out_specs=(anywhere,) * 4,
        scratch_shapes=[vm(r.shape, r.dtype) for r in results] + [dma((2, 8))],
        name="results",
    )(*results)
    return token_grad, prob_grad.T, grad_gu[None], grad_dn[None]


def solution(mesh):
    in_specs = (
        P(("expert", "dp"), None),
        P(("expert", "dp"), None),
        P(("expert", "dp"), None),
        P(("expert", "dp"), None),
        P("expert", None, None),
        P("expert", None, None),
    )
    out_specs = (
        P(("expert", "dp"), None),
        P(("expert", "dp"), None),
        P("expert", "dp", None),
        P("expert", "dp", None),
    )
    return jax.shard_map(
        on_device, mesh=mesh, in_specs=in_specs, out_specs=out_specs, check_vma=False
    )
```
